256 devices in a mesh: table: 16 (over z, core), row: 16 (over y, x).
Axes of the slice: x: 4, y: 4, z: 8, core: 2. Of those that a mesh axis runs over, the one named last changes fastest.
Arguments:
- dense_feat: bfloat16 [65536, 128], P(('table', 'row')), may hold values from -6 to 6
- pooled: bfloat16 [65536, 2048], P(('table', 'row')), may hold values from -6 to 6
- labels: int32 [65536], P(('table', 'row')), may hold values 0 or 1
- cross_down: bfloat16 [2176, 256], replicated, may hold values from -0.125 to 0.125
- cross_up: bfloat16 [256, 2176], replicated, may hold values from -0.375 to 0.375
- cross_bias: float32 [2176], replicated, may hold values from -3 to 3
- w_hidden1: bfloat16 [2176, 1024], replicated, may hold values from -0.125 to 0.125
- bias1: float32 [1024], replicated, may hold values from -3 to 3
- w_hidden2: bfloat16 [1024, 1024], replicated, may hold values from -0.1875 to 0.1875
- bias2: float32 [1024], replicated, may hold values from -3 to 3
- w_logit: float32 [1024], replicated, may hold values from -0.6 to 0.6
- lookup_slots: int32 [16, 65536, 4], P('table'), may hold values from 0 to 16383, as said below
Outputs:
- row_grads: float32 [16, 16384, 128], P('table', 'row')
- grad_cross_down: float32 [2176, 256], P('row')
- grad_cross_up: float32 [256, 2176], P('row')
- grad_cross_bias: float32 [2176], P('row')
- grad_hidden1: float32 [2176, 1024], P('row')
- grad_bias1: float32 [1024], P('row')
- grad_hidden2: float32 [1024, 1024], P('row')
- grad_bias2: float32 [1024], P('row')
- grad_logit: float32 [1024], P('row')
The draws below stay inside these ranges and needn't reach their ends.
Inputs may be any that keep to these rules, and one draw needn't show every extreme that they name: `lookup_slots`: row shard r of a table owns the slots r * 1024 to (r + 1) * 1024 - 1; a lookup's slot is the deduplicated row that it reads.
All inputs are finite; a program needn't handle non-finite values. No bound on the sum of `labels` on one device may be relied on, other than what follows from the above.
Results may differ from the reference program's by a relative error of at most 0.015.
Values may be sent and summed in bfloat16 or wider, within the bound.
A program may use at most 128 MiB of HBM per device.

```python
import jax
import jax.numpy as jnp
from jax import lax

EMB = 128
TABLES = 16
RANK = 256
HID = 1024
HOT = 4
BATCH = 65536
FEAT = 2176
U_SHARD = 1024
SLOTS = 16384
N_ROW = 16


def draw_lookup_slots(key, part):
    key = jax.random.fold_in(key, 7)
    keys = jax.random.split(key, 4)
    shape = (TABLES, BATCH, HOT)
    first = jax.random.randint(keys[0], shape, 0, N_ROW)
    second = jax.random.randint(keys[1], shape, 0, N_ROW)
    shard = jnp.maximum(first, second)
    upper = jax.random.randint(keys[2], shape, 0, U_SHARD)
    lower = jax.random.randint(keys[3], shape, 0, U_SHARD)
    within = U_SHARD - 1 - jnp.minimum(upper, lower)
    slots = shard * U_SHARD + within
    slots = slots.at[:, 0, 0].set(SLOTS - 1)
    slots = slots.at[:, 0, 1].set(0)
    return slots.astype(jnp.int32)


def touch_ends(drawn, own_key, low, high):
    longest = drawn.shape.index(max(drawn.shape))
    spots = []
    for shift in (0, 1):
        where = [jax.random.randint(jax.random.fold_in(own_key, axis), (), 0, length) for axis, length in enumerate(drawn.shape)]
        where[longest] = (where[longest] + shift) % drawn.shape[longest]
        spots.append(tuple(where))
    return drawn.at[spots[0]].set(low).at[spots[1]].set(high)


def level_of(key, shape, cuts, least, largest):
    def one(axis_at, shards_of):
        draws = jax.random.uniform(jax.random.fold_in(jax.random.fold_in(key, 6), axis_at), (shards_of,), jnp.float32, least / len(cuts), largest / len(cuts))
        return jnp.repeat(jnp.exp(draws), shape[axis_at] // shards_of).reshape((-1,) + (1,) * (len(shape) - axis_at - 1))

    level = one(*cuts[0])
    for cut in cuts[1:]:
        level = level * one(*cut)
    return level


def gaussian(key, dims, width, bound, shards=(), kind=jnp.bfloat16):
    entries = width * jax.random.normal(key, dims, jnp.float32)
    if shards:
        entries = entries * level_of(key, dims, shards, -0.22, 0.18)
    return jnp.clip(entries, -bound, bound).astype(kind)


def setup_inputs(seed: int = 0) -> dict:
    streams_of = jax.random.split(jax.random.key(seed), 13)
    dense_feat = gaussian(streams_of[0], (BATCH, EMB), 1.0, 6.0, ((0, 256),))
    pooled = gaussian(streams_of[1], (BATCH, TABLES * EMB), 1.0, 6.0, ((0, 256),))
    labels = touch_ends((jax.random.randint(streams_of[2], (BATCH,), 0, 4) < 1).astype(jnp.int32), jax.random.fold_in(streams_of[2], 1), 0, 1)
    cross_down = gaussian(streams_of[3], (FEAT, RANK), FEAT ** -0.5, 0.125)
    cross_up = gaussian(streams_of[4], (RANK, FEAT), RANK ** -0.5, 0.375)
    cross_bias = gaussian(streams_of[5], (FEAT,), 0.5, 3.0, (), jnp.float32)
    w_hidden1 = gaussian(streams_of[6], (FEAT, HID), FEAT ** -0.5, 0.125)
    bias1 = gaussian(streams_of[7], (HID,), 0.5, 3.0, (), jnp.float32)
    w_hidden2 = gaussian(streams_of[8], (HID, HID), HID ** -0.5, 0.1875)
    bias2 = gaussian(streams_of[9], (HID,), 0.5, 3.0, (), jnp.float32)
    w_logit = gaussian(streams_of[10], (HID,), 0.1, 0.6, (), jnp.float32)
    lookup_slots = draw_lookup_slots(jax.random.fold_in(streams_of[12], 71), 0)
    return {"dense_feat": dense_feat, "pooled": pooled, "labels": labels, "cross_down": cross_down, "cross_up": cross_up, "cross_bias": cross_bias, "w_hidden1": w_hidden1, "bias1": bias1, "w_hidden2": w_hidden2, "bias2": bias2, "w_logit": w_logit, "lookup_slots": lookup_slots}


loss_scale = 16.0


def swish_slope(value):
    sig = jax.nn.sigmoid(value)
    return sig * (1.0 + value * (1.0 - sig))


def dense_backward(dense_feat, pooled, labels, cross_down, cross_up, cross_bias, w_hidden1, bias1, w_hidden2, bias2, w_logit):
    stacked = jnp.concatenate([dense_feat, pooled], axis=1)
    stacked_wide = stacked.astype(jnp.float32)
    reduced = jnp.dot(stacked, cross_down, preferred_element_type=jnp.float32).astype(jnp.bfloat16)
    widened = jnp.dot(reduced, cross_up, preferred_element_type=jnp.float32) + cross_bias
    crossed = (stacked_wide * widened + stacked_wide).astype(jnp.bfloat16)
    pre_first = jnp.dot(crossed, w_hidden1, preferred_element_type=jnp.float32) + bias1
    act_first = jax.nn.silu(pre_first).astype(jnp.bfloat16)
    pre_second = jnp.dot(act_first, w_hidden2, preferred_element_type=jnp.float32) + bias2
    act_second = jax.nn.silu(pre_second).astype(jnp.bfloat16)
    act_wide = act_second.astype(jnp.float32)
    logits = jnp.sum(act_wide * w_logit, axis=1)
    delta_logit = loss_scale * (jax.nn.sigmoid(logits) - labels.astype(jnp.float32))
    delta_second = (delta_logit[:, None] * w_logit[None, :] * swish_slope(pre_second)).astype(jnp.bfloat16)
    grad_logit = jnp.sum(act_wide * delta_logit[:, None], axis=0)
    grad_hidden2 = jnp.dot(act_first.T, delta_second, preferred_element_type=jnp.float32)
    grad_bias2 = jnp.sum(delta_second.astype(jnp.float32), axis=0)
    back_first = jnp.dot(delta_second, w_hidden2.T, preferred_element_type=jnp.float32)
    delta_first = (back_first * swish_slope(pre_first)).astype(jnp.bfloat16)
    grad_hidden1 = jnp.dot(crossed.T, delta_first, preferred_element_type=jnp.float32)
    grad_bias1 = jnp.sum(delta_first.astype(jnp.float32), axis=0)
    delta_crossed = jnp.dot(delta_first, w_hidden1.T, preferred_element_type=jnp.float32)
    delta_widened = (delta_crossed * stacked_wide).astype(jnp.bfloat16)
    grad_cross_up = jnp.dot(reduced.T, delta_widened, preferred_element_type=jnp.float32)
    grad_cross_bias = jnp.sum(delta_widened.astype(jnp.float32), axis=0)
    delta_reduced = jnp.dot(delta_widened, cross_up.T, preferred_element_type=jnp.float32).astype(jnp.bfloat16)
    grad_cross_down = jnp.dot(stacked.T, delta_reduced, preferred_element_type=jnp.float32)
    delta_stacked = delta_crossed * (widened + 1.0) + jnp.dot(delta_reduced, cross_down.T, preferred_element_type=jnp.float32)
    grads = (grad_cross_down, grad_cross_up, grad_cross_bias, grad_hidden1, grad_bias1, grad_hidden2, grad_bias2, grad_logit)
    return grads, delta_stacked


def reference(dense_feat, pooled, labels, cross_down, cross_up, cross_bias, w_hidden1, bias1, w_hidden2, bias2, w_logit, lookup_slots):
    grads, delta_stacked = dense_backward(dense_feat, pooled, labels, cross_down, cross_up, cross_bias, w_hidden1, bias1, w_hidden2, bias2, w_logit)
    rounded = delta_stacked[:, EMB:].astype(jnp.bfloat16)
    rounded = lax.optimization_barrier(rounded)
    pooled_grad = rounded.astype(jnp.float32).reshape(BATCH, TABLES, EMB)
    by_table = jnp.transpose(pooled_grad, (1, 0, 2))
    values = jnp.broadcast_to(by_table[:, :, None, :], (TABLES, BATCH, HOT, EMB)).reshape(TABLES * BATCH * HOT, EMB)
    offsets = (jnp.arange(TABLES, dtype=jnp.int32) * jnp.int32(SLOTS)).astype(jnp.int32)
    flat_ids = (lookup_slots.astype(jnp.int32) + offsets[:, None, None]).astype(jnp.int32).reshape(TABLES * BATCH * HOT)
    summed = jax.ops.segment_sum(values, flat_ids, num_segments=TABLES * SLOTS)
    row_grads = summed.reshape(TABLES, SLOTS, EMB)
    return (row_grads, grads[0], grads[1], grads[2], grads[3], grads[4], grads[5], grads[6], grads[7])
```

```python
import jax
import jax.numpy as jnp
from jax import lax
from jax.experimental import pallas as pl
from jax.experimental.pallas import tpu as pltpu
from jax.sharding import PartitionSpec as P

loss_scale = 16.0


def swish_slope(value):
    sig = jax.nn.sigmoid(value)
    return sig * (1.0 + value * (1.0 - sig))


def dense_backward(
    dense_feat,
    pooled,
    labels,
    cross_down,
    cross_up,
    cross_bias,
    w_hidden1,
    bias1,
    w_hidden2,
    bias2,
    w_logit,
):
    stacked = jnp.concatenate([dense_feat, pooled], axis=1)
    stacked_wide = stacked.astype(jnp.float32)
    reduced = jnp.dot(stacked, cross_down, preferred_element_type=jnp.float32).astype(jnp.bfloat16)
    widened = jnp.dot(reduced, cross_up, preferred_element_type=jnp.float32) + cross_bias
    crossed = (stacked_wide * widened + stacked_wide).astype(jnp.bfloat16)
    pre_first = jnp.dot(crossed, w_hidden1, preferred_element_type=jnp.float32) + bias1
    act_first = jax.nn.silu(pre_first).astype(jnp.bfloat16)
    pre_second = jnp.dot(act_first, w_hidden2, preferred_element_type=jnp.float32) + bias2
    act_second = jax.nn.silu(pre_second).astype(jnp.bfloat16)
    act_wide = act_second.astype(jnp.float32)
    logits = jnp.sum(act_wide * w_logit, axis=1)
    delta_logit = loss_scale * (jax.nn.sigmoid(logits) - labels.astype(jnp.float32))
    delta_second = (delta_logit[:, None] * w_logit[None, :] * swish_slope(pre_second)).astype(
        jnp.bfloat16
    )
    grad_logit = jnp.sum(act_wide * delta_logit[:, None], axis=0)
    grad_hidden2 = jnp.dot(act_first.T, delta_second, preferred_element_type=jnp.float32)
    grad_bias2 = jnp.sum(delta_second.astype(jnp.float32), axis=0)
    back_first = jnp.dot(delta_second, w_hidden2.T, preferred_element_type=jnp.float32)
    delta_first = (back_first * swish_slope(pre_first)).astype(jnp.bfloat16)
    grad_hidden1 = jnp.dot(crossed.T, delta_first, preferred_element_type=jnp.float32)
    grad_bias1 = jnp.sum(delta_first.astype(jnp.float32), axis=0)
    delta_crossed = jnp.dot(delta_first, w_hidden1.T, preferred_element_type=jnp.float32)
    delta_widened = (delta_crossed * stacked_wide).astype(jnp.bfloat16)
    grad_cross_up = jnp.dot(reduced.T, delta_widened, preferred_element_type=jnp.float32)
    grad_cross_bias = jnp.sum(delta_widened.astype(jnp.float32), axis=0)
    delta_reduced = jnp.dot(delta_widened, cross_up.T, preferred_element_type=jnp.float32).astype(
        jnp.bfloat16
    )
    grad_cross_down = jnp.dot(stacked.T, delta_reduced, preferred_element_type=jnp.float32)
    delta_stacked = delta_crossed * (widened + 1.0) + jnp.dot(
        delta_reduced, cross_down.T, preferred_element_type=jnp.float32
    )
    grads = (
        grad_cross_down,
        grad_cross_up,
        grad_cross_bias,
        grad_hidden1,
        grad_bias1,
        grad_hidden2,
        grad_bias2,
        grad_logit,
    )
    return (grads, delta_stacked)


def scatter_kernel(s_ref, v_ref, o_ref, wide, *accs):
    count = v_ref.shape[0]
    slots, width = o_ref.shape
    unroll = 16

    def clear(i, c):
        for acc in accs:
            acc[pl.ds(pl.multiple_of(i * 256, 256), 256), :] = jnp.zeros((256, width), jnp.float32)
        return c

    lax.fori_loop(0, slots // 256, clear, 0)
    wide[...] = v_ref[...].astype(jnp.float32)

    def step(g, c):
        base = g * unroll
        for i in range(0, unroll, 2):
            row0 = wide[pl.ds(base + i, 1), :]
            row1 = wide[pl.ds(base + i + 1, 1), :]
            for which, acc in enumerate(accs):
                s0 = s_ref[which * count + base + i]
                s1 = s_ref[which * count + base + i + 1]
                old0 = acc[pl.ds(s0, 1), :]
                old1 = acc[pl.ds(s1, 1), :]
                new0 = old0 + row0
                new1 = jnp.where(s0 == s1, new0, old1) + row1
                acc[pl.ds(s0, 1), :] = new0
                acc[pl.ds(s1, 1), :] = new1
        return c

    lax.fori_loop(0, count // unroll, step, 0)

    def finish(i, c):
        at = pl.ds(pl.multiple_of(i * 128, 128), 128)
        total = accs[0][at, :]
        for acc in accs[1:]:
            total = total + acc[at, :]
        o_ref[at, :] = total.astype(o_ref.dtype)
        return c

    lax.fori_loop(0, slots // 128, finish, 0)


def scatter_rows(slots, values):
    count, width = values.shape
    total_slots = slots.size
    return pl.pallas_call(
        scatter_kernel,
        out_shape=jax.ShapeDtypeStruct((total_slots, width), jnp.bfloat16),
        in_specs=[pl.BlockSpec(memory_space=pltpu.SMEM), pl.BlockSpec(memory_space=pltpu.VMEM)],
        out_specs=pl.BlockSpec(memory_space=pltpu.VMEM),
        scratch_shapes=[pltpu.VMEM((count, width), jnp.float32)]
        + [pltpu.VMEM((total_slots, width), jnp.float32)] * (slots.size // count),
        compiler_params=pltpu.CompilerParams(vmem_limit_bytes=58 << 20),
    )(slots, values)


def local(
    dense_feat,
    pooled,
    labels,
    cross_down,
    cross_up,
    cross_bias,
    w_hidden1,
    bias1,
    w_hidden2,
    bias2,
    w_logit,
    lookup_slots,
):
    grads, delta_stacked = dense_backward(
        dense_feat,
        pooled,
        labels,
        cross_down,
        cross_up,
        cross_bias,
        w_hidden1,
        bias1,
        w_hidden2,
        bias2,
        w_logit,
    )
    batch_dev = dense_feat.shape[0]
    width = dense_feat.shape[1]
    n_table = lax.axis_size("table")
    n_row = lax.axis_size("row")
    hot_count = lookup_slots.shape[2]
    samples = n_table * batch_dev
    row_pos = lax.axis_index("row")
    pooled_grad = delta_stacked[:, width:].astype(jnp.bfloat16).reshape(batch_dev, n_table, width)
    received = lax.all_to_all(pooled_grad, "table", split_axis=1, concat_axis=0, tiled=True)
    mine = jnp.transpose(lookup_slots[0]).reshape(hot_count, n_table, n_row, batch_dev)
    mine = lax.dynamic_index_in_dim(mine, row_pos, axis=2, keepdims=False)
    partial = scatter_rows(mine.reshape(-1), received.reshape(samples, width))
    parts = partial.reshape(n_row, -1, width)
    swapped = lax.all_to_all(parts, "row", split_axis=0, concat_axis=0, tiled=True)
    row_grads = jnp.sum(swapped.astype(jnp.float32), axis=0)[None]
    flat = jnp.concatenate([g.astype(jnp.bfloat16).reshape(n_row, -1) for g in grads], axis=1)
    swapped = lax.all_to_all(flat, "row", split_axis=0, concat_axis=0, tiled=True)
    total = lax.psum(jnp.sum(swapped.astype(jnp.float32), axis=0), "table")
    outs = []
    at = 0
    for g in grads:
        shape = (g.shape[0] // n_row,) + g.shape[1:]
        size = g.size // n_row
        outs.append(total[at : at + size].reshape(shape))
        at += size
    return (row_grads, *outs)


def solution(mesh):
    in_specs = (
        P(("table", "row"), None),
        P(("table", "row"), None),
        P(("table", "row")),
        P(),
        P(),
        P(),
        P(),
        P(),
        P(),
        P(),
        P(),
        P("table", None, None),
    )
    out_specs = (
        P("table", "row", None),
        P("row", None),
        P("row", None),
        P("row"),
        P("row", None),
        P("row"),
        P("row", None),
        P("row"),
        P("row"),
    )
    return jax.shard_map(local, mesh=mesh, in_specs=in_specs, out_specs=out_specs, check_vma=False)
```

```python
import jax
import jax.numpy as jnp
from jax import lax
from jax.experimental import pallas as pl
from jax.experimental.pallas import tpu as pltpu
from jax.sharding import PartitionSpec as P

loss_scale = 16.0


def swish_slope(value):
    sig = jax.nn.sigmoid(value)
    return sig * (1.0 + value * (1.0 - sig))


def dense_path(
    dense_feat,
    pooled,
    labels,
    cross_down,
    cross_up,
    cross_bias,
    w_hidden1,
    bias1,
    w_hidden2,
    bias2,
    w_logit,
):
    stacked = jnp.concatenate([dense_feat, pooled], axis=1)
    stacked_wide = stacked.astype(jnp.float32)
    reduced = jnp.dot(stacked, cross_down, preferred_element_type=jnp.float32).astype(jnp.bfloat16)
    widened = jnp.dot(reduced, cross_up, preferred_element_type=jnp.float32) + cross_bias
    crossed = (stacked_wide * widened + stacked_wide).astype(jnp.bfloat16)
    pre_first = jnp.dot(crossed, w_hidden1, preferred_element_type=jnp.float32) + bias1
    act_first = jax.nn.silu(pre_first).astype(jnp.bfloat16)
    pre_second = jnp.dot(act_first, w_hidden2, preferred_element_type=jnp.float32) + bias2
    act_second = jax.nn.silu(pre_second).astype(jnp.bfloat16)
    act_wide = act_second.astype(jnp.float32)
    logits = jnp.sum(act_wide * w_logit, axis=1)
    delta_logit = loss_scale * (jax.nn.sigmoid(logits) - labels.astype(jnp.float32))
    delta_second = (delta_logit[:, None] * w_logit[None, :] * swish_slope(pre_second)).astype(
        jnp.bfloat16
    )
    grad_logit = jnp.sum(act_wide * delta_logit[:, None], axis=0)
    back_first = jnp.dot(delta_second, w_hidden2.T, preferred_element_type=jnp.float32)
    delta_first = (back_first * swish_slope(pre_first)).astype(jnp.bfloat16)
    delta_crossed = jnp.dot(delta_first, w_hidden1.T, preferred_element_type=jnp.float32)
    delta_widened = (delta_crossed * stacked_wide).astype(jnp.bfloat16)
    delta_reduced = jnp.dot(delta_widened, cross_up.T, preferred_element_type=jnp.float32).astype(
        jnp.bfloat16
    )
    delta_stacked = delta_crossed * (widened + 1.0) + jnp.dot(
        delta_reduced, cross_down.T, preferred_element_type=jnp.float32
    )
    saved = (
        stacked,
        crossed,
        reduced,
        act_first,
        delta_second,
        delta_first,
        delta_widened,
        delta_reduced,
        grad_logit[None, :],
    )
    return (saved, delta_stacked)


MESH = pl.DeviceIdType.MESH
X, Y, Z = 4, 4, 8
PIECE = 144
WIDE = 1024
f32, bf16 = jnp.float32, jnp.bfloat16


def place():
    table = lax.axis_index("table")
    row = lax.axis_index("row")
    core, z = lax.rem(table, 2), table // 2
    y, x = row // X, lax.rem(row, X)
    return table, row, core, z, y, x


def slot_of(half, shard, y, x):
    dy = lax.rem(shard // X - y + Y, Y)
    dx = lax.rem(lax.rem(shard, X) - x + X, X)
    return dx * 4 + dy if half == 0 else dy * 4 + dx


def shard_of(core, y, x, first, second):
    dx = first * (1 - core) + second * core
    dy = second * (1 - core) + first * core
    return lax.rem(y + dy, Y) * X + lax.rem(x + dx, X)


def transposed(dst, src):
    def move(i, c):
        at = pl.ds(pl.multiple_of(i * 128, 128), 128)
        dst[at, :] = src[:, at].T
        return c

    lax.fori_loop(0, src.shape[1] // 128, move, 0)


def weight_kernel(
    stacked,
    crossed,
    reduced,
    act_first,
    delta_second,
    delta_first,
    delta_widened,
    delta_reduced,
    grad_logit,
    out0,
    out1,
    out2,
    out3,
    packed,
    landed,
    flipped,
    small,
    send_sem,
    recv_sem,
):
    table, row, core, z, y, x = place()
    other = z * 2 + 1 - core
    barrier = pltpu.get_barrier_semaphore()
    pl.semaphore_signal(barrier, inc=1, device_id=(other, row), device_id_type=MESH)
    pl.semaphore_wait(barrier, 1)

    def copy(half, slot):
        return pltpu.make_async_remote_copy(
            src_ref=packed.at[half, slot],
            dst_ref=landed.at[slot],
            send_sem=send_sem.at[slot],
            recv_sem=recv_sem.at[slot],
            device_id=(other, row),
            device_id_type=MESH,
        )

    def dot(a, b):
        return jnp.dot(a, b, preferred_element_type=f32)

    transposed(flipped, act_first)

    def second(i, c):
        m = dot(flipped[pl.ds(pl.multiple_of(i * 256, 256), 256), :], delta_second[...])
        for k in range(4):
            packed[1, slot_of(1, i * 4 + k, y, x), 0:64, :] = m[64 * k : 64 * k + 64].astype(bf16)
        return c

    lax.fori_loop(0, 4, second, 0)

    transposed(small, reduced)

    def up(i, c):
        left = small[pl.ds(pl.multiple_of(i * 64, 64), 64), :]
        m0 = dot(left, delta_widened[:, 0:1024])
        m1 = dot(left, delta_widened[:, 1024:2048])
        m2 = dot(left, delta_widened[:, 2048:2176])
        for k in range(4):
            slot = slot_of(1, i * 4 + k, y, x)
            part = slice(16 * k, 16 * k + 16)
            packed[1, slot, 64:80, :] = m0[part].astype(bf16)
            packed[1, slot, 80:96, :] = m1[part].astype(bf16)
            packed[1, slot, 96:112, 768:896] = m2[part].astype(bf16)
            packed[1, slot, 96:112, 896:1024] = jnp.zeros((16, 128), bf16)
            packed[1, slot, 128:144, 768:1024] = jnp.zeros((16, 256), bf16)
        return c

    lax.fori_loop(0, 4, up, 0)

    transposed(flipped, stacked)

    def down(i, c):
        m = dot(flipped[pl.ds(pl.multiple_of(i * 272, 16), 272), :], delta_reduced[...])
        for k in range(2):
            slot = slot_of(1, i * 2 + k, y, x)
            d = m[136 * k : 136 * k + 136]
            packed[1, slot, 96:144, 0:256] = d[0:48].astype(bf16)
            packed[1, slot, 96:144, 256:512] = d[48:96].astype(bf16)
            last = jnp.concatenate([d[96:136], jnp.zeros((8, 256), f32)], axis=0)
            packed[1, slot, 96:144, 512:768] = last.astype(bf16)
        return c

    lax.fori_loop(0, 8, down, 0)

    ones = jnp.ones((8, 256), bf16)
    wide_sums = dot(ones, delta_widened[...])
    which = lax.broadcasted_iota(jnp.int32, (8, 1024), 0)
    sums = jnp.where(which == 1, dot(ones, delta_first[...]), dot(ones, delta_second[...]))
    sums = jnp.where(which == 3, grad_logit[...], sums)
    first_row = which[:, 0:256] == 0
    for shard in range(16):
        a = wide_sums if shard == 0 else pltpu.roll(wide_sums, 2176 - 136 * shard, 1)
        b = sums if shard == 0 else pltpu.roll(sums, 1024 - 64 * shard, 1)
        block = jnp.where(first_row, a[:, 0:256], b[:, 0:256])
        block = jnp.concatenate([block, jnp.zeros((8, 256), f32)], axis=0).astype(bf16)
        packed[1, slot_of(1, shard, y, x), 112:128, 768:1024] = block

    @pl.when(core == 0)
    def _():
        def send(slot, c):
            copy(1, slot).start()
            return c

        lax.fori_loop(0, 16, send, 0)

    transposed(flipped, crossed)

    def first(i, c):
        m = dot(flipped[pl.ds(pl.multiple_of(i * 272, 16), 272), :], delta_first[...])
        for k in range(2):
            slot = slot_of(0, i * 2 + k, y, x)
            d = jnp.concatenate([m[136 * k : 136 * k + 136], jnp.zeros((8, WIDE), f32)], axis=0)
            packed[0, slot] = d.astype(bf16)

            @pl.when(core == 1)
            def _():
                copy(0, slot).start()

        return c

    lax.fori_loop(0, 8, first, 0)

    for shift, out in enumerate((out0, out1, out2, out3)):

        def add(i, c):
            slot = shift * 4 + i
            copy(1 - core, slot).wait_recv()
            out[i] = (packed[core, slot].astype(f32) + landed[slot].astype(f32)).astype(bf16)
            return c

        lax.fori_loop(0, 4, add, 0)

    def drain(slot, c):
        copy(1 - core, slot).wait_send()
        return c

    lax.fori_loop(0, 16, drain, 0)


def weight_grads(saved):
    vmem = pl.BlockSpec(memory_space=pltpu.VMEM)
    piece = jax.ShapeDtypeStruct((4, PIECE, WIDE), bf16)
    return pl.pallas_call(
        weight_kernel,
        out_shape=(piece,) * 4,
        in_specs=[vmem] * 9,
        out_specs=(vmem,) * 4,
        scratch_shapes=[
            pltpu.VMEM((2, 16, PIECE, WIDE), bf16),
            pltpu.VMEM((16, PIECE, WIDE), bf16),
            pltpu.VMEM((2176, 256), bf16),
            pltpu.VMEM((256, 256), bf16),
            pltpu.SemaphoreType.DMA((16,)),
            pltpu.SemaphoreType.DMA((16,)),
        ],
        compiler_params=pltpu.CompilerParams(
            collective_id=0, has_side_effects=True, vmem_limit_bytes=48 << 20
        ),
        cost_estimate=pl.CostEstimate(
            flops=2_300_000_000, bytes_accessed=60_000_000, transcendentals=0
        ),
    )(*saved)


def exchange_kernel(
    parts,
    s0,
    s1,
    s2,
    s3,
    row_out,
    h1_out,
    h2_out,
    up_out,
    down_out,
    vec_out,
    own,
    got1,
    mid,
    got2,
    dense,
    dense_mid,
    dense_got,
    zparts,
    zgot,
    final,
    local_sem,
    send1,
    recv1,
    send2,
    recv2,
    wsend,
    wrecv,
    zsend,
    zrecv,
    gsend,
    grecv,
    csend,
    crecv,
):
    table, row, core, z, y, x = place()
    sibling = z * 2 + 1 - core

    def first_peer(d):
        return (table, shard_of(core, y, x, d, 0))

    def second_peer(j):
        return (table, shard_of(core, y, x, 0, j))

    def z_peer(d):
        return (lax.rem(z + d, Z) * 2 + core, row)

    def remote(src, dst, s, r, who):
        return pltpu.make_async_remote_copy(
            src_ref=src, dst_ref=dst, send_sem=s, recv_sem=r, device_id=who, device_id_type=MESH
        )

    barrier = pltpu.get_barrier_semaphore()
    peers = [first_peer(d) for d in (1, 2, 3)] + [second_peer(j) for j in (1, 2, 3)]
    peers += [z_peer(d) for d in range(1, Z)] + [(sibling, row)]
    for who in peers:
        pl.semaphore_signal(barrier, inc=1, device_id=who, device_id_type=MESH)
    pl.semaphore_wait(barrier, len(peers))

    def copy1(d, j):
        return remote(
            parts.at[shard_of(core, y, x, d, j)],
            got1.at[d - 1, j],
            send1.at[d - 1, j],
            recv1.at[d - 1, j],
            first_peer(d),
        )

    def copy2(j):
        return remote(mid.at[j - 1], got2.at[j - 1], send2.at[j - 1], recv2.at[j - 1], second_peer(j))

    def copyw(j):
        return remote(
            dense_mid.at[j - 1], dense_got.at[j - 1], wsend.at[j - 1], wrecv.at[j - 1], second_peer(j)
        )

    def copyz(d):
        return remote(
            zparts.at[lax.rem(z + d, Z)], zgot.at[d - 1], zsend.at[d - 1], zrecv.at[d - 1], z_peer(d)
        )

    def copyg(d, which):
        piece = final.at[core, which]
        return remote(piece, piece, gsend.at[d - 1], grecv.at[d - 1], z_peer(d))

    def copyc(half):
        return remote(final.at[half], final.at[half], csend, crecv, (sibling, row))

    def local_dense(d):
        return pltpu.make_async_copy((s0, s1, s2, s3)[d], dense.at[d], local_sem.at[d])

    def local_own(j):
        return pltpu.make_async_copy(
            parts.at[shard_of(core, y, x, 0, j)], own.at[j], local_sem.at[4 + j]
        )

    for d in range(4):
        local_dense(d).start()
    for j in (1, 2, 3, 0):
        for d in (1, 2, 3):
            copy1(d, j).start()
    for j in range(4):
        local_own(j).start()
    for d in range(4):
        local_dense(d).wait()

    def dense_sum(j, at):
        total = dense[0, j, at, :].astype(f32)
        for d in (1, 2, 3):
            total = total + dense[d, j, at, :].astype(f32)
        return total

    for j in (1, 2, 3):

        def dense_block(i, c):
            at = pl.ds(pl.multiple_of(i * 16, 16), 16)
            dense_mid[j - 1, at, :] = dense_sum(j, at).astype(bf16)
            return c

        lax.fori_loop(0, PIECE // 16, dense_block, 0)
        copyw(j).start()
    for j in range(4):
        local_own(j).wait()
    for j in (1, 2, 3):
        copyw(j).wait_recv()

    def dense_last(i, c):
        at = pl.ds(pl.multiple_of(i * 16, 16), 16)
        total = dense_sum(0, at)
        for j in (1, 2, 3):
            total = total + dense_got[j - 1, at, :].astype(f32)
        total = total.astype(bf16)
        for k in range(Z):
            zparts[k, at, :] = total[:, 128 * k : 128 * k + 128]
        return c

    lax.fori_loop(0, PIECE // 16, dense_last, 0)
    for d in range(1, Z):
        copyz(d).start()

    def row_sum(j, at):
        total = own[j, at, :].astype(f32)
        for d in (1, 2, 3):
            total = total + got1[d - 1, j, at, :].astype(f32)
        return total

    def row_mid(j):
        for d in (1, 2, 3):
            copy1(d, j).wait_recv()

        def block(i, c):
            at = pl.ds(pl.multiple_of(i * 128, 128), 128)
            mid[j - 1, at, :] = row_sum(j, at).astype(bf16)
            return c

        lax.fori_loop(0, 8, block, 0)
        copy2(j).start()

    row_mid(1)
    for d in range(1, Z):
        copyz(d).wait_recv()
    total = zparts[z].astype(f32)
    for d in range(1, Z):
        total = total + zgot[d - 1].astype(f32)
    final[core, z] = total.astype(bf16)
    for d in range(1, Z):
        copyg(d, z).start()
    row_mid(2)
    for d in range(1, Z):
        copyg(d, lax.rem(z - d + Z, Z)).wait_recv()
    copyc(core).start()
    row_mid(3)
    for d in (1, 2, 3):
        copy1(d, 0).wait_recv()
    copyc(1 - core).wait_recv()
    for k in range(Z):
        at = slice(128 * k, 128 * k + 128)
        h1_out[:, at] = final[0, k, :, :].astype(f32)[0:136]
        h2_out[:, at] = final[1, k, 0:64, :].astype(f32)
        up_out[:, at] = final[1, k, 64:80, :].astype(f32)
        up_out[:, 1024 + 128 * k : 1024 + 128 * k + 128] = final[1, k, 80:96, :].astype(f32)
    up_out[:, 2048:2176] = final[1, 6, 96:112, :].astype(f32)
    for k in range(2):
        at = slice(128 * k, 128 * k + 128)
        down_out[0:48, at] = final[1, k, 96:144, :].astype(f32)
        down_out[48:96, at] = final[1, 2 + k, 96:144, :].astype(f32)
        down_out[96:136, at] = final[1, 4 + k, 96:144, :].astype(f32)[0:40]
        vec_out[:, at] = final[1, 6 + k, 112:128, :].astype(f32)[0:8]
    for j in (1, 2, 3):
        copy2(j).wait_recv()

    def row_last(i, c):
        at = pl.ds(pl.multiple_of(i * 128, 128), 128)
        total = row_sum(0, at)
        for j in (1, 2, 3):
            total = total + got2[j - 1, at, :].astype(f32)
        row_out[at, :] = total
        return c

    lax.fori_loop(0, 8, row_last, 0)

    for d in (1, 2, 3):
        for j in range(4):
            copy1(d, j).wait_send()
    for j in (1, 2, 3):
        copy2(j).wait_send()
        copyw(j).wait_send()
    for d in range(1, Z):
        copyz(d).wait_send()
        copyg(d, z).wait_send()
    copyc(core).wait_send()


def exchange(parts, sums):
    vmem = pl.BlockSpec(memory_space=pltpu.VMEM)
    anywhere = pl.BlockSpec(memory_space=pl.ANY)
    rows, width = parts.shape[1:]
    dma = pltpu.SemaphoreType.DMA
    return pl.pallas_call(
        exchange_kernel,
        out_shape=(
            jax.ShapeDtypeStruct((rows, width), f32),
            jax.ShapeDtypeStruct((136, 1024), f32),
            jax.ShapeDtypeStruct((64, 1024), f32),
            jax.ShapeDtypeStruct((16, 2176), f32),
            jax.ShapeDtypeStruct((136, 256), f32),
            jax.ShapeDtypeStruct((8, 256), f32),
        ),
        in_specs=[anywhere] * 5,
        out_specs=(vmem,) * 6,
        scratch_shapes=[
            pltpu.VMEM((4, rows, width), bf16),
            pltpu.VMEM((3, 4, rows, width), bf16),
            pltpu.VMEM((3, rows, width), bf16),
            pltpu.VMEM((3, rows, width), bf16),
            pltpu.VMEM((4, 4, PIECE, WIDE), bf16),
            pltpu.VMEM((3, PIECE, WIDE), bf16),
            pltpu.VMEM((3, PIECE, WIDE), bf16),
            pltpu.VMEM((Z, PIECE, 128), bf16),
            pltpu.VMEM((Z - 1, PIECE, 128), bf16),
            pltpu.VMEM((2, Z, PIECE, 128), bf16),
            dma((8,)),
            dma((3, 4)),
            dma((3, 4)),
            dma((3,)),
            dma((3,)),
            dma((3,)),
            dma((3,)),
            dma((Z - 1,)),
            dma((Z - 1,)),
            dma((Z - 1,)),
            dma((Z - 1,)),
            dma,
            dma,
        ],
        compiler_params=pltpu.CompilerParams(
            collective_id=1, has_side_effects=True, vmem_limit_bytes=48 << 20
        ),
    )(parts, *sums)


def first_axis_pairs(shift):
    pairs = []
    for table in range(2 * Z):
        for row in range(Y * X):
            y, x = row // X, row % X
            if table % 2 == 0:
                x = (x + shift) % X
            else:
                y = (y + shift) % Y
            pairs.append((table * Y * X + row, table * Y * X + y * X + x))
    return pairs


def scatter_kernel(s_ref, v_ref, o_ref, wide, *accs):
    count = v_ref.shape[0]
    slots, width = o_ref.shape
    unroll = 16

    def clear(i, c):
        for acc in accs:
            acc[pl.ds(pl.multiple_of(i * 256, 256), 256), :] = jnp.zeros((256, width), jnp.float32)
        return c

    lax.fori_loop(0, slots // 256, clear, 0)
    wide[...] = v_ref[...].astype(jnp.float32)

    def step(g, c):
        base = g * unroll
        for i in range(0, unroll, 2):
            row0 = wide[pl.ds(base + i, 1), :]
            row1 = wide[pl.ds(base + i + 1, 1), :]
            for which, acc in enumerate(accs):
                s0 = s_ref[which * count + base + i]
                s1 = s_ref[which * count + base + i + 1]
                old0 = acc[pl.ds(s0, 1), :]
                old1 = acc[pl.ds(s1, 1), :]
                new0 = old0 + row0
                new1 = jnp.where(s0 == s1, new0, old1) + row1
                acc[pl.ds(s0, 1), :] = new0
                acc[pl.ds(s1, 1), :] = new1
        return c

    lax.fori_loop(0, count // unroll, step, 0)

    def finish(i, c):
        at = pl.ds(pl.multiple_of(i * 128, 128), 128)
        total = accs[0][at, :]
        for acc in accs[1:]:
            total = total + acc[at, :]
        o_ref[at, :] = total.astype(o_ref.dtype)
        return c

    lax.fori_loop(0, slots // 128, finish, 0)


def scatter_rows(slots, values):
    count, width = values.shape
    total_slots = slots.size
    return pl.pallas_call(
        scatter_kernel,
        out_shape=jax.ShapeDtypeStruct((total_slots, width), jnp.bfloat16),
        in_specs=[pl.BlockSpec(memory_space=pltpu.SMEM), pl.BlockSpec(memory_space=pltpu.VMEM)],
        out_specs=pl.BlockSpec(memory_space=pltpu.VMEM),
        scratch_shapes=[pltpu.VMEM((count, width), jnp.float32)]
        + [pltpu.VMEM((total_slots, width), jnp.float32)] * (slots.size // count),
        compiler_params=pltpu.CompilerParams(vmem_limit_bytes=58 << 20),
        cost_estimate=pl.CostEstimate(
            flops=10_000_000, bytes_accessed=100_000_000, transcendentals=0
        ),
    )(slots, values)


def local(
    dense_feat,
    pooled,
    labels,
    cross_down,
    cross_up,
    cross_bias,
    w_hidden1,
    bias1,
    w_hidden2,
    bias2,
    w_logit,
    lookup_slots,
):
    saved, delta_stacked = dense_path(
        dense_feat,
        pooled,
        labels,
        cross_down,
        cross_up,
        cross_bias,
        w_hidden1,
        bias1,
        w_hidden2,
        bias2,
        w_logit,
    )
    batch_dev = dense_feat.shape[0]
    width = dense_feat.shape[1]
    n_table = lax.axis_size("table")
    n_row = lax.axis_size("row")
    hot_count = lookup_slots.shape[2]
    samples = n_table * batch_dev
    row_pos = lax.axis_index("row")
    pooled_grad = delta_stacked[:, width:].astype(jnp.bfloat16).reshape(batch_dev, n_table, width)
    saved, pooled_grad = lax.optimization_barrier((saved, pooled_grad))
    received = lax.all_to_all(pooled_grad, "table", split_axis=1, concat_axis=0, tiled=True)
    mine = jnp.transpose(lookup_slots[0]).reshape(hot_count, n_table, n_row, batch_dev)
    mine = lax.dynamic_index_in_dim(mine, row_pos, axis=2, keepdims=False)
    kept, *away = weight_grads(saved)
    came = [
        lax.ppermute(part, ("table", "row"), first_axis_pairs(shift + 1))
        for shift, part in enumerate(away)
    ]
    partial = scatter_rows(mine.reshape(-1), received.reshape(samples, width))
    row_grads, g_h1, g_h2, g_up, g_down, vecs = exchange(
        partial.reshape(n_row, -1, width), [kept] + came
    )
    return (
        row_grads[None],
        g_down,
        g_up,
        vecs[0, 0:136],
        g_h1,
        vecs[1, 0:64],
        g_h2,
        vecs[2, 0:64],
        vecs[3, 0:64],
    )


def solution(mesh):
    in_specs = (
        P(("table", "row"), None),
        P(("table", "row"), None),
        P(("table", "row")),
        P(),
        P(),
        P(),
        P(),
        P(),
        P(),
        P(),
        P(),
        P("table", None, None),
    )
    out_specs = (
        P("table", "row", None),
        P("row", None),
        P("row", None),
        P("row"),
        P("row", None),
        P("row"),
        P("row", None),
        P("row"),
        P("row"),
    )
    return jax.shard_map(local, mesh=mesh, in_specs=in_specs, out_specs=out_specs, check_vma=False)
```

```python
import jax
import jax.numpy as jnp
from jax import lax
from jax.experimental import pallas as pl
from jax.experimental.pallas import tpu as pltpu
from jax.sharding import PartitionSpec as P

loss_scale = 16.0


def swish_slope(value):
    sig = jax.nn.sigmoid(value)
    return sig * (1.0 + value * (1.0 - sig))


def dense_path(
    dense_feat,
    pooled,
    labels,
    cross_down,
    cross_up,
    cross_bias,
    w_hidden1,
    bias1,
    w_hidden2,
    bias2,
    w_logit,
):
    stacked = jnp.concatenate([dense_feat, pooled], axis=1)
    stacked_wide = stacked.astype(jnp.float32)
    reduced = jnp.dot(stacked, cross_down, preferred_element_type=jnp.float32).astype(jnp.bfloat16)
    widened = jnp.dot(reduced, cross_up, preferred_element_type=jnp.float32) + cross_bias
    crossed = (stacked_wide * widened + stacked_wide).astype(jnp.bfloat16)
    pre_first = jnp.dot(crossed, w_hidden1, preferred_element_type=jnp.float32) + bias1
    act_first = jax.nn.silu(pre_first).astype(jnp.bfloat16)
    pre_second = jnp.dot(act_first, w_hidden2, preferred_element_type=jnp.float32) + bias2
    act_second = jax.nn.silu(pre_second).astype(jnp.bfloat16)
    act_wide = act_second.astype(jnp.float32)
    logits = jnp.sum(act_wide * w_logit, axis=1)
    delta_logit = loss_scale * (jax.nn.sigmoid(logits) - labels.astype(jnp.float32))
    delta_second = (delta_logit[:, None] * w_logit[None, :] * swish_slope(pre_second)).astype(
        jnp.bfloat16
    )
    grad_logit = jnp.sum(act_wide * delta_logit[:, None], axis=0)
    back_first = jnp.dot(delta_second, w_hidden2.T, preferred_element_type=jnp.float32)
    delta_first = (back_first * swish_slope(pre_first)).astype(jnp.bfloat16)
    delta_crossed = jnp.dot(delta_first, w_hidden1.T, preferred_element_type=jnp.float32)
    delta_widened = (delta_crossed * stacked_wide).astype(jnp.bfloat16)
    delta_reduced = jnp.dot(delta_widened, cross_up.T, preferred_element_type=jnp.float32).astype(
        jnp.bfloat16
    )
    delta_stacked = delta_crossed * (widened + 1.0) + jnp.dot(
        delta_reduced, cross_down.T, preferred_element_type=jnp.float32
    )
    saved = (
        stacked,
        crossed,
        reduced,
        act_first,
        delta_second,
        delta_first,
        delta_widened,
        delta_reduced,
        grad_logit[None, :],
    )
    return (saved, delta_stacked)


MESH = pl.DeviceIdType.MESH
X, Y, Z = 4, 4, 8
PIECE = 144
WIDE = 1024
f32, bf16 = jnp.float32, jnp.bfloat16


def place():
    table = lax.axis_index("table")
    row = lax.axis_index("row")
    core, z = lax.rem(table, 2), table // 2
    y, x = row // X, lax.rem(row, X)
    return table, row, core, z, y, x


def slot_of(half, shard, y, x):
    dy = lax.rem(shard // X - y + Y, Y)
    dx = lax.rem(lax.rem(shard, X) - x + X, X)
    return dx * 4 + dy if half == 0 else dy * 4 + dx


def shard_of(core, y, x, first, second):
    dx = first * (1 - core) + second * core
    dy = second * (1 - core) + first * core
    return lax.rem(y + dy, Y) * X + lax.rem(x + dx, X)


def transposed(dst, src):
    def move(i, c):
        at = pl.ds(pl.multiple_of(i * 128, 128), 128)
        dst[at, :] = src[:, at].T
        return c

    lax.fori_loop(0, src.shape[1] // 128, move, 0)


def weight_kernel(
    stacked,
    crossed,
    reduced,
    act_first,
    delta_second,
    delta_first,
    delta_widened,
    delta_reduced,
    grad_logit,
    out0,
    out1,
    out2,
    out3,
    packed,
    landed,
    flipped,
    small,
    send_sem,
    recv_sem,
):
    table, row, core, z, y, x = place()
    other = z * 2 + 1 - core
    barrier = pltpu.get_barrier_semaphore()
    pl.semaphore_signal(barrier, inc=1, device_id=(other, row), device_id_type=MESH)
    pl.semaphore_wait(barrier, 1)

    def copy(half, slot):
        return pltpu.make_async_remote_copy(
            src_ref=packed.at[half, slot],
            dst_ref=landed.at[slot],
            send_sem=send_sem.at[slot],
            recv_sem=recv_sem.at[slot],
            device_id=(other, row),
            device_id_type=MESH,
        )

    def dot(a, b):
        return jnp.dot(a, b, preferred_element_type=f32)

    transposed(flipped, act_first)

    def second(i, c):
        m = dot(flipped[pl.ds(pl.multiple_of(i * 256, 256), 256), :], delta_second[...])
        for k in range(4):
            packed[1, slot_of(1, i * 4 + k, y, x), 0:64, :] = m[64 * k : 64 * k + 64].astype(bf16)
        return c

    lax.fori_loop(0, 4, second, 0)

    transposed(small, reduced)

    def up(i, c):
        left = small[pl.ds(pl.multiple_of(i * 64, 64), 64), :]
        m0 = dot(left, delta_widened[:, 0:1024])
        m1 = dot(left, delta_widened[:, 1024:2048])
        m2 = dot(left, delta_widened[:, 2048:2176])
        for k in range(4):
            slot = slot_of(1, i * 4 + k, y, x)
            part = slice(16 * k, 16 * k + 16)
            packed[1, slot, 64:80, :] = m0[part].astype(bf16)
            packed[1, slot, 80:96, :] = m1[part].astype(bf16)
            packed[1, slot, 96:112, 768:896] = m2[part].astype(bf16)
            packed[1, slot, 96:112, 896:1024] = jnp.zeros((16, 128), bf16)
            packed[1, slot, 128:144, 768:1024] = jnp.zeros((16, 256), bf16)
        return c

    lax.fori_loop(0, 4, up, 0)

    transposed(flipped, stacked)

    def down(i, c):
        m = dot(flipped[pl.ds(pl.multiple_of(i * 272, 16), 272), :], delta_reduced[...])
        for k in range(2):
            slot = slot_of(1, i * 2 + k, y, x)
            d = m[136 * k : 136 * k + 136]
            packed[1, slot, 96:144, 0:256] = d[0:48].astype(bf16)
            packed[1, slot, 96:144, 256:512] = d[48:96].astype(bf16)
            last = jnp.concatenate([d[96:136], jnp.zeros((8, 256), f32)], axis=0)
            packed[1, slot, 96:144, 512:768] = last.astype(bf16)
        return c

    lax.fori_loop(0, 8, down, 0)

    ones = jnp.ones((8, 256), bf16)
    wide_sums = dot(ones, delta_widened[...])
    which = lax.broadcasted_iota(jnp.int32, (8, 1024), 0)
    sums = jnp.where(which == 1, dot(ones, delta_first[...]), dot(ones, delta_second[...]))
    sums = jnp.where(which == 3, grad_logit[...], sums)
    first_row = which[:, 0:256] == 0
    for shard in range(16):
        a = wide_sums if shard == 0 else pltpu.roll(wide_sums, 2176 - 136 * shard, 1)
        b = sums if shard == 0 else pltpu.roll(sums, 1024 - 64 * shard, 1)
        block = jnp.where(first_row, a[:, 0:256], b[:, 0:256])
        block = jnp.concatenate([block, jnp.zeros((8, 256), f32)], axis=0).astype(bf16)
        packed[1, slot_of(1, shard, y, x), 112:128, 768:1024] = block

    @pl.when(core == 0)
    def _():
        def send(slot, c):
            copy(1, slot).start()
            return c

        lax.fori_loop(0, 16, send, 0)

    transposed(flipped, crossed)

    def first(i, c):
        m = dot(flipped[pl.ds(pl.multiple_of(i * 272, 16), 272), :], delta_first[...])
        for k in range(2):
            slot = slot_of(0, i * 2 + k, y, x)
            d = jnp.concatenate([m[136 * k : 136 * k + 136], jnp.zeros((8, WIDE), f32)], axis=0)
            packed[0, slot] = d.astype(bf16)

            @pl.when(core == 1)
            def _():
                copy(0, slot).start()

        return c

    lax.fori_loop(0, 8, first, 0)

    for shift, out in enumerate((out0, out1, out2, out3)):

        def add(i, c):
            slot = shift * 4 + i
            copy(1 - core, slot).wait_recv()
            out[i] = (packed[core, slot].astype(f32) + landed[slot].astype(f32)).astype(bf16)
            return c

        lax.fori_loop(0, 4, add, 0)

    def drain(slot, c):
        copy(1 - core, slot).wait_send()
        return c

    lax.fori_loop(0, 16, drain, 0)


def weight_grads(saved):
    vmem = pl.BlockSpec(memory_space=pltpu.VMEM)
    piece = jax.ShapeDtypeStruct((4, PIECE, WIDE), bf16)
    return pl.pallas_call(
        weight_kernel,
        out_shape=(piece,) * 4,
        in_specs=[vmem] * 9,
        out_specs=(vmem,) * 4,
        scratch_shapes=[
            pltpu.VMEM((2, 16, PIECE, WIDE), bf16),
            pltpu.VMEM((16, PIECE, WIDE), bf16),
            pltpu.VMEM((2176, 256), bf16),
            pltpu.VMEM((256, 256), bf16),
            pltpu.SemaphoreType.DMA((16,)),
            pltpu.SemaphoreType.DMA((16,)),
        ],
        compiler_params=pltpu.CompilerParams(
            collective_id=0, has_side_effects=True, vmem_limit_bytes=48 << 20
        ),
        cost_estimate=pl.CostEstimate(
            flops=2_300_000_000, bytes_accessed=60_000_000, transcendentals=0
        ),
    )(*saved)


def exchange_kernel(
    parts,
    s0,
    s1,
    s2,
    s3,
    row_out,
    h1_out,
    h2_out,
    up_out,
    down_out,
    vec_out,
    via_plus,
    via_minus,
    acc_plus,
    acc_minus,
    got_plus,
    got_minus,
    mid,
    via2,
    got2,
    dense,
    dense_mid,
    dense_via_plus,
    dense_via_minus,
    dense_got,
    zparts,
    zgot,
    final,
    local_sem,
    send1,
    recv1,
    send2,
    recv2,
    wsend,
    wrecv,
    zsend,
    zrecv,
    gsend,
    grecv,
    csend,
    crecv,
):
    table, row, core, z, y, x = place()
    sibling = z * 2 + 1 - core
    rows = parts.shape[1]

    def first_peer(d):
        return (table, shard_of(core, y, x, d, 0))

    def second_peer(j):
        return (table, shard_of(core, y, x, 0, j))

    def z_peer(d):
        return (lax.rem(z + d, Z) * 2 + core, row)

    def remote(src, dst, s, r, who):
        return pltpu.make_async_remote_copy(
            src_ref=src, dst_ref=dst, send_sem=s, recv_sem=r, device_id=who, device_id_type=MESH
        )

    barrier = pltpu.get_barrier_semaphore()
    peers = [first_peer(1), first_peer(3), second_peer(1), second_peer(3)]
    peers += [z_peer(d) for d in range(1, Z)] + [(sibling, row)]
    for who in peers:
        pl.semaphore_signal(barrier, inc=1, device_id=who, device_id_type=MESH)
    pl.semaphore_wait(barrier, len(peers))

    def ring(chunk, cut, size, vias, accs, gots, send, recv, plus, minus):
        low, high = pl.ds(0, cut), pl.ds(cut, size - cut)
        pairs = (
            (chunk(2).at[low], vias[0], plus),
            (chunk(2).at[high], vias[1], minus),
            (chunk(1).at[high], gots[0].at[high], plus),
            (chunk(3).at[low], gots[1].at[low], minus),
            (accs[0], gots[0].at[low], plus),
            (accs[1], gots[1].at[high], minus),
        )

        def copy(k):
            src, dst, who = pairs[k]
            return remote(src, dst, send.at[k], recv.at[k], who)

        return copy

    half = rows // 2

    def ring1(j):
        return ring(
            lambda d: parts.at[shard_of(core, y, x, d, j)],
            half,
            rows,
            (via_plus.at[j], via_minus.at[j]),
            (acc_plus.at[j], acc_minus.at[j]),
            (got_plus.at[j], got_minus.at[j]),
            send1.at[j],
            recv1.at[j],
            first_peer(1),
            first_peer(3),
        )

    def ring2():
        return ring(
            lambda d: mid.at[d],
            half,
            rows,
            (via2.at[0], via2.at[1]),
            (mid.at[1, pl.ds(0, half)], mid.at[3, pl.ds(half, half)]),
            (got2.at[0], got2.at[1]),
            send2,
            recv2,
            second_peer(1),
            second_peer(3),
        )

    cut = 80

    def ringw():
        return ring(
            lambda d: dense_mid.at[d],
            cut,
            PIECE,
            (dense_via_plus, dense_via_minus),
            (dense_mid.at[1, pl.ds(0, cut)], dense_mid.at[3, pl.ds(cut, PIECE - cut)]),
            (dense_got.at[0], dense_got.at[1]),
            wsend,
            wrecv,
            second_peer(1),
            second_peer(3),
        )

    def go(copies, *which):
        for k in which:
            copies(k).start()

    def arrived(copies, *which):
        for k in which:
            copies(k).wait_recv()

    def copyz(d):
        return remote(
            zparts.at[lax.rem(z + d, Z)], zgot.at[d - 1], zsend.at[d - 1], zrecv.at[d - 1], z_peer(d)
        )

    def copyg(d, which):
        piece = final.at[core, which]
        return remote(piece, piece, gsend.at[d - 1], grecv.at[d - 1], z_peer(d))

    def copyc(half):
        return remote(final.at[half], final.at[half], csend, crecv, (sibling, row))

    def local_dense(d):
        return pltpu.make_async_copy((s0, s1, s2, s3)[d], dense.at[d], local_sem.at[d])

    def forward(j):
        to_plus, to_minus = shard_of(core, y, x, 1, j), shard_of(core, y, x, 3, j)
        copies = ring1(j)
        arrived(copies, 0, 1)

        def block(i, c):
            at = pl.ds(pl.multiple_of(i * 128, 128), 128)
            later = pl.ds(pl.multiple_of(half + i * 128, 128), 128)
            acc_plus[j, at, :] = (
                parts[to_plus, at, :].astype(f32) + via_plus[j, at, :].astype(f32)
            ).astype(bf16)
            acc_minus[j, at, :] = (
                parts[to_minus, later, :].astype(f32) + via_minus[j, at, :].astype(f32)
            ).astype(bf16)
            return c

        lax.fori_loop(0, half // 128, block, 0)
        go(copies, 4, 5)

    def row_mid(j):
        arrived(ring1(j), 2, 3, 4, 5)
        mine = shard_of(core, y, x, 0, j)

        def block(i, c):
            at = pl.ds(pl.multiple_of(i * 128, 128), 128)
            total = parts[mine, at, :].astype(f32)
            total = total + got_plus[j, at, :].astype(f32) + got_minus[j, at, :].astype(f32)
            mid[j, at, :] = total.astype(bf16)
            return c

        lax.fori_loop(0, rows // 128, block, 0)

    go(ring1(2), 0, 1)
    for d in range(4):
        local_dense(d).start()
    go(ring1(2), 2, 3)
    go(ring1(1), 0, 1)
    for d in range(4):
        local_dense(d).wait()

    for j in (2, 1, 3, 0):

        def dense_block(i, c):
            at = pl.ds(pl.multiple_of(i * 16, 16), 16)
            total = dense[0, j, at, :].astype(f32)
            for d in (1, 2, 3):
                total = total + dense[d, j, at, :].astype(f32)
            dense_mid[j, at, :] = total.astype(bf16)
            return c

        lax.fori_loop(0, PIECE // 16, dense_block, 0)
        if j == 2:
            go(ringw(), 0, 1)
            forward(2)
            go(ring1(1), 2, 3)
            go(ring1(3), 0, 1)
        elif j != 0:
            go(ringw(), 2 if j == 1 else 3)
    arrived(ringw(), 0, 1)
    for target, came, start, count in (
        (1, dense_via_plus, 0, cut),
        (3, dense_via_minus, cut, PIECE - cut),
    ):

        def dense_add(i, c):
            at = pl.ds(pl.multiple_of(i * 16, 16), 16)
            to = pl.ds(pl.multiple_of(start + i * 16, 16), 16)
            dense_mid[target, to, :] = (
                dense_mid[target, to, :].astype(f32) + came[at, :].astype(f32)
            ).astype(bf16)
            return c

        lax.fori_loop(0, count // 16, dense_add, 0)
    go(ringw(), 4, 5)
    forward(1)
    go(ring1(3), 2, 3)
    go(ring1(0), 0, 1)
    forward(3)
    go(ring1(0), 2, 3)

    arrived(ringw(), 2, 3, 4, 5)

    def dense_last(i, c):
        at = pl.ds(pl.multiple_of(i * 16, 16), 16)
        total = dense_mid[0, at, :].astype(f32)
        total = total + dense_got[0, at, :].astype(f32) + dense_got[1, at, :].astype(f32)
        total = total.astype(bf16)
        for k in range(Z):
            zparts[k, at, :] = total[:, 128 * k : 128 * k + 128]
        return c

    lax.fori_loop(0, PIECE // 16, dense_last, 0)
    for d in range(1, Z):
        copyz(d).start()

    row_mid(2)
    go(ring2(), 0, 1)
    forward(0)
    for d in range(1, Z):
        copyz(d).wait_recv()
    total = zparts[z].astype(f32)
    for d in range(1, Z):
        total = total + zgot[d - 1].astype(f32)
    final[core, z] = total.astype(bf16)
    for d in range(1, Z):
        copyg(d, z).start()
    row_mid(1)
    go(ring2(), 2)
    row_mid(3)
    go(ring2(), 3)
    arrived(ring2(), 0, 1)

    def mid_add(i, c):
        at = pl.ds(pl.multiple_of(i * 128, 128), 128)
        later = pl.ds(pl.multiple_of(half + i * 128, 128), 128)
        mid[1, at, :] = (mid[1, at, :].astype(f32) + via2[0, at, :].astype(f32)).astype(bf16)
        mid[3, later, :] = (mid[3, later, :].astype(f32) + via2[1, at, :].astype(f32)).astype(bf16)
        return c

    lax.fori_loop(0, half // 128, mid_add, 0)
    go(ring2(), 4, 5)
    for d in range(1, Z):
        copyg(d, lax.rem(z - d + Z, Z)).wait_recv()
    copyc(core).start()
    arrived(ring1(0), 2, 3, 4, 5)
    copyc(1 - core).wait_recv()
    for k in range(Z):
        at = slice(128 * k, 128 * k + 128)
        h1_out[:, at] = final[0, k, :, :].astype(f32)[0:136]
        h2_out[:, at] = final[1, k, 0:64, :].astype(f32)
        up_out[:, at] = final[1, k, 64:80, :].astype(f32)
        up_out[:, 1024 + 128 * k : 1024 + 128 * k + 128] = final[1, k, 80:96, :].astype(f32)
    up_out[:, 2048:2176] = final[1, 6, 96:112, :].astype(f32)
    for k in range(2):
        at = slice(128 * k, 128 * k + 128)
        down_out[0:48, at] = final[1, k, 96:144, :].astype(f32)
        down_out[48:96, at] = final[1, 2 + k, 96:144, :].astype(f32)
        down_out[96:136, at] = final[1, 4 + k, 96:144, :].astype(f32)[0:40]
        vec_out[:, at] = final[1, 6 + k, 112:128, :].astype(f32)[0:8]
    arrived(ring2(), 2, 3, 4, 5)

    own = shard_of(core, y, x, 0, 0)

    def row_last(i, c):
        at = pl.ds(pl.multiple_of(i * 128, 128), 128)
        total = parts[own, at, :].astype(f32)
        total = total + got_plus[0, at, :].astype(f32) + got_minus[0, at, :].astype(f32)
        row_out[at, :] = total + got2[0, at, :].astype(f32) + got2[1, at, :].astype(f32)
        return c

    lax.fori_loop(0, rows // 128, row_last, 0)

    for j in range(4):
        for k in range(6):
            ring1(j)(k).wait_send()
    for k in range(6):
        ring2()(k).wait_send()
        ringw()(k).wait_send()
    for d in range(1, Z):
        copyz(d).wait_send()
        copyg(d, z).wait_send()
    copyc(core).wait_send()


def exchange(parts, sums):
    vmem = pl.BlockSpec(memory_space=pltpu.VMEM)
    anywhere = pl.BlockSpec(memory_space=pl.ANY)
    rows, width = parts.shape[1:]
    half = rows // 2
    dma = pltpu.SemaphoreType.DMA
    return pl.pallas_call(
        exchange_kernel,
        out_shape=(
            jax.ShapeDtypeStruct((rows, width), f32),
            jax.ShapeDtypeStruct((136, 1024), f32),
            jax.ShapeDtypeStruct((64, 1024), f32),
            jax.ShapeDtypeStruct((16, 2176), f32),
            jax.ShapeDtypeStruct((136, 256), f32),
            jax.ShapeDtypeStruct((8, 256), f32),
        ),
        in_specs=[vmem] + [anywhere] * 4,
        out_specs=(vmem,) * 6,
        scratch_shapes=[
            pltpu.VMEM((4, half, width), bf16),
            pltpu.VMEM((4, half, width), bf16),
            pltpu.VMEM((4, half, width), bf16),
            pltpu.VMEM((4, half, width), bf16),
            pltpu.VMEM((4, rows, width), bf16),
            pltpu.VMEM((4, rows, width), bf16),
            pltpu.VMEM((4, rows, width), bf16),
            pltpu.VMEM((2, half, width), bf16),
            pltpu.VMEM((2, rows, width), bf16),
            pltpu.VMEM((4, 4, PIECE, WIDE), bf16),
            pltpu.VMEM((4, PIECE, WIDE), bf16),
            pltpu.VMEM((80, WIDE), bf16),
            pltpu.VMEM((64, WIDE), bf16),
            pltpu.VMEM((2, PIECE, WIDE), bf16),
            pltpu.VMEM((Z, PIECE, 128), bf16),
            pltpu.VMEM((Z - 1, PIECE, 128), bf16),
            pltpu.VMEM((2, Z, PIECE, 128), bf16),
            dma((4,)),
            dma((4, 6)),
            dma((4, 6)),
            dma((6,)),
            dma((6,)),
            dma((6,)),
            dma((6,)),
            dma((Z - 1,)),
            dma((Z - 1,)),
            dma((Z - 1,)),
            dma((Z - 1,)),
            dma,
            dma,
        ],
        compiler_params=pltpu.CompilerParams(
            collective_id=1, has_side_effects=True, vmem_limit_bytes=44 << 20
        ),
    )(parts, *sums)


def first_axis_pairs(shift):
    pairs = []
    for table in range(2 * Z):
        for row in range(Y * X):
            y, x = row // X, row % X
            if table % 2 == 0:
                x = (x + shift) % X
            else:
                y = (y + shift) % Y
            pairs.append((table * Y * X + row, table * Y * X + y * X + x))
    return pairs


def scatter_kernel(slots_ref, v_ref, o_ref, s_ref, wide, sem, *accs):
    count = v_ref.shape[0]
    slots, width = o_ref.shape
    row = lax.axis_index("row")
    per_table = slots_ref.shape[1] // (2 * Z)
    own = per_table // (Y * X)

    def fetch(t):
        at = (t // 2) * per_table + row * own + (t % 2) * 128
        return pltpu.make_async_copy(
            slots_ref.at[:, pl.ds(pl.multiple_of(at, 128), 128)], s_ref.at[t], sem.at[t]
        )

    for t in range(count // 128):
        fetch(t).start()

    def clear(i, c):
        for acc in accs:
            acc[pl.ds(pl.multiple_of(i * 256, 256), 256), :] = jnp.zeros((256, width), f32)
        return c

    lax.fori_loop(0, slots // 256, clear, 0)
    wide[...] = v_ref[...].astype(f32)
    for t in range(count // 128):
        fetch(t).wait()

    def step(g, c):
        for i in range(0, 128, 2):
            row0 = wide[pl.ds(g * 128 + i, 1), :]
            row1 = wide[pl.ds(g * 128 + i + 1, 1), :]
            for which, acc in enumerate(accs):
                slot0 = s_ref[g, which, i]
                slot1 = s_ref[g, which, i + 1]
                old0 = acc[pl.ds(slot0, 1), :]
                old1 = acc[pl.ds(slot1, 1), :]
                new0 = old0 + row0
                new1 = jnp.where(slot0 == slot1, new0, old1) + row1
                acc[pl.ds(slot0, 1), :] = new0
                acc[pl.ds(slot1, 1), :] = new1
        return c

    lax.fori_loop(0, count // 128, step, 0)

    def finish(i, c):
        at = pl.ds(pl.multiple_of(i * 128, 128), 128)
        total = accs[0][at, :]
        for acc in accs[1:]:
            total = total + acc[at, :]
        o_ref[at, :] = total.astype(o_ref.dtype)
        return c

    lax.fori_loop(0, slots // 128, finish, 0)


def scatter_rows(slots, values, total_slots):
    count, width = values.shape
    hot = slots.shape[0]
    return pl.pallas_call(
        scatter_kernel,
        out_shape=jax.ShapeDtypeStruct((total_slots, width), bf16),
        in_specs=[pl.BlockSpec(memory_space=pl.ANY), pl.BlockSpec(memory_space=pltpu.VMEM)],
        out_specs=pl.BlockSpec(memory_space=pltpu.VMEM),
        scratch_shapes=[
            pltpu.SMEM((count // 128, hot, 128), jnp.int32),
            pltpu.VMEM((count, width), f32),
            pltpu.SemaphoreType.DMA((count // 128,)),
        ]
        + [pltpu.VMEM((total_slots, width), f32)] * hot,
        compiler_params=pltpu.CompilerParams(vmem_limit_bytes=44 << 20),
        cost_estimate=pl.CostEstimate(
            flops=10_000_000, bytes_accessed=100_000_000, transcendentals=0
        ),
    )(slots, values)


def local(
    dense_feat,
    pooled,
    labels,
    cross_down,
    cross_up,
    cross_bias,
    w_hidden1,
    bias1,
    w_hidden2,
    bias2,
    w_logit,
    lookup_slots,
):
    saved, delta_stacked = dense_path(
        dense_feat,
        pooled,
        labels,
        cross_down,
        cross_up,
        cross_bias,
        w_hidden1,
        bias1,
        w_hidden2,
        bias2,
        w_logit,
    )
    batch_dev = dense_feat.shape[0]
    width = dense_feat.shape[1]
    n_table = lax.axis_size("table")
    n_row = lax.axis_size("row")
    samples = n_table * batch_dev
    u_shard = 1024
    pooled_grad = delta_stacked[:, width:].astype(jnp.bfloat16).reshape(batch_dev, n_table, width)
    saved, pooled_grad = lax.optimization_barrier((saved, pooled_grad))
    received = lax.all_to_all(pooled_grad, "table", split_axis=1, concat_axis=0, tiled=True)
    kept, *away = weight_grads(saved)
    came = [
        lax.ppermute(part, ("table", "row"), first_axis_pairs(shift + 1))
        for shift, part in enumerate(away)
    ]
    partial = scatter_rows(
        jnp.transpose(lookup_slots[0]), received.reshape(samples, width), n_row * u_shard
    )
    row_grads, g_h1, g_h2, g_up, g_down, vecs = exchange(
        partial.reshape(n_row, -1, width), [kept] + came
    )
    return (
        row_grads[None],
        g_down,
        g_up,
        vecs[0, 0:136],
        g_h1,
        vecs[1, 0:64],
        g_h2,
        vecs[2, 0:64],
        vecs[3, 0:64],
    )


def solution(mesh):
    in_specs = (
        P(("table", "row"), None),
        P(("table", "row"), None),
        P(("table", "row")),
        P(),
        P(),
        P(),
        P(),
        P(),
        P(),
        P(),
        P(),
        P("table", None, None),
    )
    out_specs = (
        P("table", "row", None),
        P("row", None),
        P("row", None),
        P("row"),
        P("row", None),
        P("row"),
        P("row", None),
        P("row"),
        P("row"),
    )
    return jax.shard_map(local, mesh=mesh, in_specs=in_specs, out_specs=out_specs, check_vma=False)
```

```python
import jax
import jax.numpy as jnp
from jax import lax
from jax.experimental import pallas as pl
from jax.experimental.pallas import tpu as pltpu
from jax.sharding import PartitionSpec as P

loss_scale = 16.0


MESH = pl.DeviceIdType.MESH
X, Y, Z = 4, 4, 8
PIECE = 144
WIDE = 1024
f32, bf16 = jnp.float32, jnp.bfloat16


def place():
    table = lax.axis_index("table")
    row = lax.axis_index("row")
    core, z = lax.rem(table, 2), table // 2
    y, x = row // X, lax.rem(row, X)
    return table, row, core, z, y, x


def slot_of(half, shard, y, x):
    dy = lax.rem(shard // X - y + Y, Y)
    dx = lax.rem(lax.rem(shard, X) - x + X, X)
    return dx * 4 + dy if half == 0 else dy * 4 + dx


def shard_of(core, y, x, first, second):
    dx = first * (1 - core) + second * core
    dy = second * (1 - core) + first * core
    return lax.rem(y + dy, Y) * X + lax.rem(x + dx, X)


def transposed(dst, src):
    for i in range(src.shape[1] // 128):
        at = slice(128 * i, 128 * i + 128)
        dst[at, :] = src[:, at].T


def ring(chunk, cut, size, vias, accs, gots, send, recv, plus, minus):
    low, high = pl.ds(0, cut), pl.ds(cut, size - cut)
    pairs = (
        (lambda: chunk(2).at[low], vias[0], plus),
        (lambda: chunk(2).at[high], vias[1], minus),
        (lambda: chunk(1).at[high], gots[0].at[high], plus),
        (lambda: chunk(3).at[low], gots[1].at[low], minus),
        (lambda: accs[0], gots[0].at[low], plus),
        (lambda: accs[1], gots[1].at[high], minus),
    )

    def copy(k):
        src, dst, who = pairs[k]
        return remote(src(), dst, send.at[k], recv.at[k], who)

    return copy


def remote(src, dst, s, r, who):
    return pltpu.make_async_remote_copy(
        src_ref=src, dst_ref=dst, send_sem=s, recv_sem=r, device_id=who, device_id_type=MESH
    )


def go(copies, *which):
    for k in which:
        copies(k).start()


def arrived(copies, *which):
    for k in which:
        copies(k).wait_recv()


def dot(a, b):
    return jnp.dot(a, b, preferred_element_type=f32)


def dot_t(a, b):
    return lax.dot_general(a, b, (((1,), (1,)), ((), ())), preferred_element_type=f32)


def tiles(body, width):
    for i in range(width // 256):
        body(slice(256 * i, 256 * i + 256), i)
    if width % 256:
        body(slice(width - width % 256, width), width // 256)


def dense_kernel(
    dense_feat,
    pooled,
    cross_down,
    cross_up,
    w_hidden1,
    w_hidden2,
    labels,
    cross_bias,
    bias1,
    bias2,
    w_logit,
    received,
    out,
    stacked,
    down_w,
    up_w,
    w1,
    w2,
    wide_plus,
    crossed,
    slope1,
    slope2,
    act_first,
    act_second,
    delta_second,
    delta_first,
    delta_crossed,
    delta_widened,
    reduced,
    delta_reduced,
    grad_logit,
    ready,
    packed,
    landed,
    flipped,
    small,
    via_plus,
    via_minus,
    got_plus,
    got_minus,
    load_sem,
    tsend,
    trecv,
    send_sem,
    recv_sem,
    send1,
    recv1,
    own_sem,
):
    table, row, core, z, y, x = place()
    n_table = 2 * Z
    other = z * 2 + 1 - core

    loads = [
        pltpu.make_async_copy(dense_feat, stacked.at[:, pl.ds(0, 128)], load_sem.at[0]),
        pltpu.make_async_copy(pooled, stacked.at[:, pl.ds(128, 2048)], load_sem.at[1]),
        pltpu.make_async_copy(cross_down, down_w, load_sem.at[2]),
        pltpu.make_async_copy(cross_up, up_w, load_sem.at[3]),
    ]
    for k in range(4):
        part = pl.ds(544 * k, 544)
        loads.append(pltpu.make_async_copy(w_hidden1.at[part], w1.at[part], load_sem.at[4 + k]))
    for k in range(2):
        part = pl.ds(512 * k, 512)
        loads.append(pltpu.make_async_copy(w_hidden2.at[part], w2.at[part], load_sem.at[8 + k]))
    for one in loads:
        one.start()

    def first_peer(d):
        return (table, shard_of(core, y, x, d, 0))

    barrier = pltpu.get_barrier_semaphore()
    for d in range(1, n_table):
        who = (lax.rem(table + d, n_table), row)
        pl.semaphore_signal(barrier, inc=1, device_id=who, device_id_type=MESH)
    for d in (1, 3):
        pl.semaphore_signal(barrier, inc=1, device_id=first_peer(d), device_id_type=MESH)

    def exchange_table(d):
        to = lax.rem(table + d, n_table)
        return remote(
            ready.at[to + 1], received.at[table], tsend.at[d - 1], trecv.at[d - 1], (to, row)
        )

    def came_table(d):
        came = lax.rem(table - d + n_table, n_table)
        return remote(
            ready.at[came + 1], received.at[came], tsend.at[d - 1], trecv.at[d - 1], (came, row)
        )

    def own_table():
        return pltpu.make_async_copy(ready.at[table + 1], received.at[table], own_sem)

    for k in (0, 1, 2):
        loads[k].wait()
    reduced[...] = dot(stacked[...], down_w[...]).astype(bf16)
    loads[3].wait()

    def cross(at, i):
        widened = dot(reduced[...], up_w[:, at]) + cross_bias[:, at]
        base = stacked[:, at].astype(f32)
        crossed[:, at] = (base * widened + base).astype(bf16)
        wide_plus[:, at] = widened + 1.0

    tiles(cross, 2176)
    for k in range(4, 8):
        loads[k].wait()

    def first_layer(at, i):
        pre = dot(crossed[...], w1[:, at]) + bias1[:, at]
        sig = jax.nn.sigmoid(pre)
        act_first[:, at] = (pre * sig).astype(bf16)
        slope1[:, at] = sig * (1.0 + pre * (1.0 - sig))

    tiles(first_layer, 1024)
    for k in range(8, 10):
        loads[k].wait()

    def second_layer(at, logits):
        pre = dot(act_first[...], w2[:, at]) + bias2[:, at]
        sig = jax.nn.sigmoid(pre)
        act = (pre * sig).astype(bf16)
        act_second[:, at] = act
        slope2[:, at] = sig * (1.0 + pre * (1.0 - sig))
        return logits + jnp.sum(act.astype(f32) * w_logit[:, at], axis=1, keepdims=True)

    logits = jnp.zeros((256, 1), f32)
    for i in range(1024 // 256):
        logits = second_layer(slice(256 * i, 256 * i + 256), logits)
    same = lax.broadcasted_iota(jnp.int32, (256, 256), 0) == lax.broadcasted_iota(
        jnp.int32, (256, 256), 1
    )
    label = jnp.sum(jnp.where(same, labels[...].astype(f32), 0.0), axis=1, keepdims=True)
    delta_logit = loss_scale * (jax.nn.sigmoid(logits) - label)

    def back_second(at, i):
        delta_second[:, at] = (delta_logit * w_logit[:, at] * slope2[:, at]).astype(bf16)
        grad_logit[:, at] = jnp.sum(
            act_second[:, at].astype(f32) * delta_logit, axis=0, keepdims=True
        )

    tiles(back_second, 1024)

    def back_first(at, i):
        back = dot_t(delta_second[...], w2[at, :])
        delta_first[:, at] = (back * slope1[:, at]).astype(bf16)

    tiles(back_first, 1024)

    def back_cross(at, i):
        delta = dot_t(delta_first[...], w1[at, :])
        delta_crossed[:, at] = delta
        delta_widened[:, at] = (delta * stacked[:, at].astype(f32)).astype(bf16)

    tiles(back_cross, 2176)
    delta_reduced[...] = dot_t(delta_widened[...], up_w[...]).astype(bf16)

    def back_stacked(at, i):
        delta = delta_crossed[:, at] * wide_plus[:, at] + dot_t(delta_reduced[...], down_w[at, :])
        for k in range(delta.shape[1] // 128):
            ready[2 * i + k] = delta[:, 128 * k : 128 * k + 128].astype(bf16)

    tiles(back_stacked, 2176)
    pl.semaphore_wait(barrier, n_table + 1)
    for d in range(1, n_table):
        exchange_table(d).start()
    own_table().start()

    def copy(half, slot):
        return remote(
            packed.at[half, slot], landed.at[slot], send_sem.at[slot], recv_sem.at[slot], (other, row)
        )

    transposed(flipped, act_first)

    def second(i, c):
        m = dot(flipped[slice(256 * i, 256 * i + 256), :], delta_second[...])
        for k in range(4):
            packed[1, slot_of(1, i * 4 + k, y, x), 0:64, :] = m[64 * k : 64 * k + 64].astype(bf16)
        return c

    for i in range(4):
        second(i, 0)

    transposed(small, reduced)

    def up(i, c):
        left = small[slice(64 * i, 64 * i + 64), :]
        m0 = dot(left, delta_widened[:, 0:1024])
        m1 = dot(left, delta_widened[:, 1024:2048])
        m2 = dot(left, delta_widened[:, 2048:2176])
        for k in range(4):
            slot = slot_of(1, i * 4 + k, y, x)
            part = slice(16 * k, 16 * k + 16)
            packed[1, slot, 64:80, :] = m0[part].astype(bf16)
            packed[1, slot, 80:96, :] = m1[part].astype(bf16)
            packed[1, slot, 96:112, 768:896] = m2[part].astype(bf16)
            packed[1, slot, 96:112, 896:1024] = jnp.zeros((16, 128), bf16)
            packed[1, slot, 128:144, 768:1024] = jnp.zeros((16, 256), bf16)
        return c

    for i in range(4):
        up(i, 0)

    transposed(flipped, stacked)

    def down(i, c):
        m = dot(flipped[slice(272 * i, 272 * i + 272), :], delta_reduced[...])
        for k in range(2):
            slot = slot_of(1, i * 2 + k, y, x)
            d = m[136 * k : 136 * k + 136]
            packed[1, slot, 96:144, 0:256] = d[0:48].astype(bf16)
            packed[1, slot, 96:144, 256:512] = d[48:96].astype(bf16)
            last = jnp.concatenate([d[96:136], jnp.zeros((8, 256), f32)], axis=0)
            packed[1, slot, 96:144, 512:768] = last.astype(bf16)
        return c

    for i in range(8):
        down(i, 0)

    ones = jnp.ones((8, 256), bf16)
    wide_sums = dot(ones, delta_widened[...])
    which = lax.broadcasted_iota(jnp.int32, (8, 1024), 0)
    sums = jnp.where(which == 1, dot(ones, delta_first[...]), dot(ones, delta_second[...]))
    sums = jnp.where(which == 3, grad_logit[...], sums)
    first_row = which[:, 0:256] == 0
    for shard in range(16):
        a = wide_sums if shard == 0 else pltpu.roll(wide_sums, 2176 - 136 * shard, 1)
        b = sums if shard == 0 else pltpu.roll(sums, 1024 - 64 * shard, 1)
        block = jnp.where(first_row, a[:, 0:256], b[:, 0:256])
        block = jnp.concatenate([block, jnp.zeros((8, 256), f32)], axis=0).astype(bf16)
        packed[1, slot_of(1, shard, y, x), 112:128, 768:1024] = block

    order = (8, 9, 10, 11, 4, 12, 5, 13, 6, 14, 7, 15, 0, 1, 2, 3)

    @pl.when(core == 0)
    def _():
        for slot in order:
            copy(1, slot).start()

    transposed(flipped, crossed)

    def first(i, c):
        m = dot(flipped[slice(272 * i, 272 * i + 272), :], delta_first[...])
        for k in range(2):
            slot = slot_of(0, i * 2 + k, y, x)
            d = jnp.concatenate([m[136 * k : 136 * k + 136], jnp.zeros((8, WIDE), f32)], axis=0)
            packed[0, slot] = d.astype(bf16)
        return c

    for i in range(8):
        first(i, 0)

    @pl.when(core == 1)
    def _():
        for slot in order:
            copy(0, slot).start()

    cut = 80

    def ring1(j):
        return ring(
            lambda d: packed.at[core, d * 4 + j],
            cut,
            PIECE,
            (via_plus.at[j], via_minus.at[j]),
            (packed.at[core, 4 + j, pl.ds(0, cut)], packed.at[core, 12 + j, pl.ds(cut, PIECE - cut)]),
            (got_plus.at[j], got_minus.at[j]),
            send1.at[j],
            recv1.at[j],
            first_peer(1),
            first_peer(3),
        )

    def add_pair(slot):
        copy(1 - core, slot).wait_recv()
        packed[core, slot] = (packed[core, slot].astype(f32) + landed[slot].astype(f32)).astype(bf16)

    def go_far(j, c):
        add_pair(8 + j)
        go(ring1(j), 0, 1)
        return c

    lax.fori_loop(0, 4, go_far, 0)

    def go_near(j, c):
        add_pair(4 + j)
        go(ring1(j), 2)
        add_pair(12 + j)
        go(ring1(j), 3)
        return c

    lax.fori_loop(0, 4, go_near, 0)

    def go_on(j, c):
        arrived(ring1(j), 0, 1)
        low, high = pl.ds(0, cut), pl.ds(cut, PIECE - cut)
        packed[core, 4 + j, low] = (
            packed[core, 4 + j, low].astype(f32) + via_plus[j].astype(f32)
        ).astype(bf16)
        packed[core, 12 + j, high] = (
            packed[core, 12 + j, high].astype(f32) + via_minus[j].astype(f32)
        ).astype(bf16)
        go(ring1(j), 4, 5)
        return c

    lax.fori_loop(0, 4, go_on, 0)

    def keep(j, c):
        add_pair(j)
        return c

    lax.fori_loop(0, 4, keep, 0)

    def finish(j, c):
        arrived(ring1(j), 2, 3, 4, 5)
        total = packed[core, j].astype(f32) + got_plus[j].astype(f32) + got_minus[j].astype(f32)
        out[j] = total.astype(bf16)
        return c

    lax.fori_loop(0, 4, finish, 0)

    def drain(slot, c):
        copy(1 - core, slot).wait_send()
        return c

    lax.fori_loop(0, 16, drain, 0)

    def drain1(j, c):
        for k in range(6):
            ring1(j)(k).wait_send()
        return c

    lax.fori_loop(0, 4, drain1, 0)
    own_table().wait()
    for d in range(1, n_table):
        came_table(d).wait_recv()
        exchange_table(d).wait_send()


def dense_part(big, rows):
    vmem = pl.BlockSpec(memory_space=pltpu.VMEM)
    anywhere = pl.BlockSpec(memory_space=pl.ANY)
    n_table = 2 * Z
    dma = pltpu.SemaphoreType.DMA
    return pl.pallas_call(
        dense_kernel,
        out_shape=(
            jax.ShapeDtypeStruct((n_table, 256, 128), bf16),
            jax.ShapeDtypeStruct((4, PIECE, WIDE), bf16),
        ),
        in_specs=[anywhere] * 6 + [vmem] * 5,
        out_specs=(anywhere, vmem),
        scratch_shapes=[
            pltpu.VMEM((256, 2176), bf16),
            pltpu.VMEM((2176, 256), bf16),
            pltpu.VMEM((256, 2176), bf16),
            pltpu.VMEM((2176, 1024), bf16),
            pltpu.VMEM((1024, 1024), bf16),
            pltpu.VMEM((256, 2176), f32),
            pltpu.VMEM((256, 2176), bf16),
            pltpu.VMEM((256, 1024), f32),
            pltpu.VMEM((256, 1024), f32),
            pltpu.VMEM((256, 1024), bf16),
            pltpu.VMEM((256, 1024), bf16),
            pltpu.VMEM((256, 1024), bf16),
            pltpu.VMEM((256, 1024), bf16),
            pltpu.VMEM((256, 2176), f32),
            pltpu.VMEM((256, 2176), bf16),
            pltpu.VMEM((256, 256), bf16),
            pltpu.VMEM((256, 256), bf16),
            pltpu.VMEM((1, 1024), f32),
            pltpu.VMEM((n_table + 1, 256, 128), bf16),
            pltpu.VMEM((2, 16, PIECE, WIDE), bf16),
            pltpu.VMEM((16, PIECE, WIDE), bf16),
            pltpu.VMEM((2176, 256), bf16),
            pltpu.VMEM((256, 256), bf16),
            pltpu.VMEM((4, 80, WIDE), bf16),
            pltpu.VMEM((4, 64, WIDE), bf16),
            pltpu.VMEM((4, PIECE, WIDE), bf16),
            pltpu.VMEM((4, PIECE, WIDE), bf16),
            dma((10,)),
            dma((n_table - 1,)),
            dma((n_table - 1,)),
            dma((16,)),
            dma((16,)),
            dma((4, 6)),
            dma((4, 6)),
            dma,
        ],
        compiler_params=pltpu.CompilerParams(
            collective_id=0, has_side_effects=True, vmem_limit_bytes=58 << 20
        ),
    )(*big, *rows)


def blocks(count, size, body):
    for i in range(count):
        body(slice(i * size, i * size + size))


def exchange_kernel(
    parts,
    dense_mid,
    row_out,
    h1_out,
    h2_out,
    up_out,
    down_out,
    vec_out,
    via_plus,
    via_minus,
    acc_plus,
    acc_minus,
    got_plus,
    got_minus,
    mid,
    via2,
    got2,
    dense_via_plus,
    dense_via_minus,
    dense_acc_plus,
    dense_acc_minus,
    dense_got,
    zparts,
    zgot,
    final,
    send1,
    recv1,
    send2,
    recv2,
    wsend,
    wrecv,
    zsend,
    zrecv,
    gsend,
    grecv,
    csend,
    crecv,
):
    table, row, core, z, y, x = place()
    sibling = z * 2 + 1 - core
    rows = parts.shape[1]

    def first_peer(d):
        return (table, shard_of(core, y, x, d, 0))

    def second_peer(j):
        return (table, shard_of(core, y, x, 0, j))

    def z_peer(d):
        return (lax.rem(z + d, Z) * 2 + core, row)

    barrier = pltpu.get_barrier_semaphore()
    peers = [first_peer(1), first_peer(3), second_peer(1), second_peer(3)]
    peers += [z_peer(d) for d in range(1, Z)] + [(sibling, row)]
    for who in peers:
        pl.semaphore_signal(barrier, inc=1, device_id=who, device_id_type=MESH)
    pl.semaphore_wait(barrier, len(peers))

    half = rows // 2

    def ring1(j):
        return ring(
            lambda d: parts.at[shard_of(core, y, x, d, j)],
            half,
            rows,
            (via_plus.at[j], via_minus.at[j]),
            (acc_plus.at[j], acc_minus.at[j]),
            (got_plus.at[j], got_minus.at[j]),
            send1.at[j],
            recv1.at[j],
            first_peer(1),
            first_peer(3),
        )

    def ring2():
        return ring(
            lambda d: mid.at[d],
            half,
            rows,
            (via2.at[0], via2.at[1]),
            (mid.at[1, pl.ds(0, half)], mid.at[3, pl.ds(half, half)]),
            (got2.at[0], got2.at[1]),
            send2,
            recv2,
            second_peer(1),
            second_peer(3),
        )

    cut = 80

    def ringw():
        return ring(
            lambda d: dense_mid.at[d],
            cut,
            PIECE,
            (dense_via_plus, dense_via_minus),
            (dense_acc_plus, dense_acc_minus),
            (dense_got.at[0], dense_got.at[1]),
            wsend,
            wrecv,
            second_peer(1),
            second_peer(3),
        )

    def copyz(d):
        return remote(
            zparts.at[lax.rem(z + d, Z)], zgot.at[d - 1], zsend.at[d - 1], zrecv.at[d - 1], z_peer(d)
        )

    def copyg(d, which):
        piece = final.at[core, which]
        return remote(piece, piece, gsend.at[d - 1], grecv.at[d - 1], z_peer(d))

    def copyc(half):
        return remote(final.at[half], final.at[half], csend, crecv, (sibling, row))

    def add_up(*terms):
        total = terms[0].astype(f32)
        for term in terms[1:]:
            total = total + term.astype(f32)
        return total

    def forward(j):
        to_plus, to_minus = shard_of(core, y, x, 1, j), shard_of(core, y, x, 3, j)
        copies = ring1(j)
        arrived(copies, 0)

        def plus(at):
            acc_plus[j, at, :] = add_up(parts[to_plus, at, :], via_plus[j, at, :]).astype(bf16)

        blocks(half // 128, 128, plus)
        go(copies, 4)
        arrived(copies, 1)

        def minus(at):
            later = slice(half + at.start, half + at.stop)
            acc_minus[j, at, :] = add_up(parts[to_minus, later, :], via_minus[j, at, :]).astype(bf16)

        blocks(half // 128, 128, minus)
        go(copies, 5)

    def row_mid(j):
        arrived(ring1(j), 2, 3, 4, 5)
        mine = shard_of(core, y, x, 0, j)

        def block(at):
            total = add_up(parts[mine, at, :], got_plus[j, at, :], got_minus[j, at, :])
            mid[j, at, :] = total.astype(bf16)

        blocks(rows // 128, 128, block)

    go(ringw(), 0, 1)
    go(ring1(2), 0, 1)
    go(ringw(), 2, 3)
    go(ring1(2), 2, 3)
    go(ring1(1), 0, 1)
    arrived(ringw(), 0, 1)

    def dense_plus(at):
        dense_acc_plus[at, :] = add_up(dense_mid[1, at, :], dense_via_plus[at, :]).astype(bf16)

    def dense_minus(at):
        later = slice(cut + at.start, cut + at.stop)
        dense_acc_minus[at, :] = add_up(dense_mid[3, later, :], dense_via_minus[at, :]).astype(bf16)

    blocks(cut // 16, 16, dense_plus)
    blocks((PIECE - cut) // 16, 16, dense_minus)
    go(ringw(), 4, 5)
    forward(2)
    go(ring1(1), 2, 3)
    go(ring1(3), 0, 1)
    forward(1)
    go(ring1(3), 2, 3)
    go(ring1(0), 0, 1)
    arrived(ringw(), 2, 3, 4, 5)

    def dense_last(at):
        total = add_up(dense_mid[0, at, :], dense_got[0, at, :], dense_got[1, at, :]).astype(bf16)
        for k in range(Z):
            zparts[k, at, :] = total[:, 128 * k : 128 * k + 128]

    blocks(PIECE // 16, 16, dense_last)
    for d in range(1, Z):
        copyz(d).start()
    forward(3)
    go(ring1(0), 2, 3)
    for d in range(1, Z):
        copyz(d).wait_recv()
    final[core, z] = add_up(zparts[z], *[zgot[d - 1] for d in range(1, Z)]).astype(bf16)
    for d in range(1, Z):
        copyg(d, z).start()
    row_mid(2)
    go(ring2(), 0, 1)
    forward(0)
    row_mid(1)
    go(ring2(), 2)
    for d in range(1, Z):
        copyg(d, lax.rem(z - d + Z, Z)).wait_recv()
    copyc(core).start()
    row_mid(3)
    go(ring2(), 3)
    arrived(ring2(), 0, 1)

    def mid_add(at):
        later = slice(half + at.start, half + at.stop)
        mid[1, at, :] = add_up(mid[1, at, :], via2[0, at, :]).astype(bf16)
        mid[3, later, :] = add_up(mid[3, later, :], via2[1, at, :]).astype(bf16)

    blocks(half // 128, 128, mid_add)
    go(ring2(), 4, 5)
    copyc(1 - core).wait_recv()
    for k in range(Z):
        at = slice(128 * k, 128 * k + 128)
        h1_out[:, at] = final[0, k, :, :].astype(f32)[0:136]
        h2_out[:, at] = final[1, k, 0:64, :].astype(f32)
        up_out[:, at] = final[1, k, 64:80, :].astype(f32)
        up_out[:, 1024 + 128 * k : 1024 + 128 * k + 128] = final[1, k, 80:96, :].astype(f32)
    up_out[:, 2048:2176] = final[1, 6, 96:112, :].astype(f32)
    for k in range(2):
        at = slice(128 * k, 128 * k + 128)
        down_out[0:48, at] = final[1, k, 96:144, :].astype(f32)
        down_out[48:96, at] = final[1, 2 + k, 96:144, :].astype(f32)
        down_out[96:136, at] = final[1, 4 + k, 96:144, :].astype(f32)[0:40]
        vec_out[:, at] = final[1, 6 + k, 112:128, :].astype(f32)[0:8]
    arrived(ring1(0), 2, 3, 4, 5)
    arrived(ring2(), 2, 3, 4, 5)

    own = shard_of(core, y, x, 0, 0)

    def row_last(at):
        row_out[at, :] = add_up(
            parts[own, at, :],
            got_plus[0, at, :],
            got_minus[0, at, :],
            got2[0, at, :],
            got2[1, at, :],
        )

    blocks(rows // 128, 128, row_last)

    for j in range(4):
        for k in range(6):
            ring1(j)(k).wait_send()
    for k in range(6):
        ring2()(k).wait_send()
        ringw()(k).wait_send()
    for d in range(1, Z):
        copyz(d).wait_send()
        copyg(d, z).wait_send()
    copyc(core).wait_send()


def exchange(parts, sums):
    vmem = pl.BlockSpec(memory_space=pltpu.VMEM)
    rows, width = parts.shape[1:]
    half = rows // 2
    dma = pltpu.SemaphoreType.DMA
    return pl.pallas_call(
        exchange_kernel,
        out_shape=(
            jax.ShapeDtypeStruct((rows, width), f32),
            jax.ShapeDtypeStruct((136, 1024), f32),
            jax.ShapeDtypeStruct((64, 1024), f32),
            jax.ShapeDtypeStruct((16, 2176), f32),
            jax.ShapeDtypeStruct((136, 256), f32),
            jax.ShapeDtypeStruct((8, 256), f32),
        ),
        in_specs=[vmem] * 2,
        out_specs=(vmem,) * 6,
        scratch_shapes=[
            pltpu.VMEM((4, half, width), bf16),
            pltpu.VMEM((4, half, width), bf16),
            pltpu.VMEM((4, half, width), bf16),
            pltpu.VMEM((4, half, width), bf16),
            pltpu.VMEM((4, rows, width), bf16),
            pltpu.VMEM((4, rows, width), bf16),
            pltpu.VMEM((4, rows, width), bf16),
            pltpu.VMEM((2, half, width), bf16),
            pltpu.VMEM((2, rows, width), bf16),
            pltpu.VMEM((80, WIDE), bf16),
            pltpu.VMEM((64, WIDE), bf16),
            pltpu.VMEM((80, WIDE), bf16),
            pltpu.VMEM((64, WIDE), bf16),
            pltpu.VMEM((2, PIECE, WIDE), bf16),
            pltpu.VMEM((Z, PIECE, 128), bf16),
            pltpu.VMEM((Z - 1, PIECE, 128), bf16),
            pltpu.VMEM((2, Z, PIECE, 128), bf16),
            dma((4, 6)),
            dma((4, 6)),
            dma((6,)),
            dma((6,)),
            dma((6,)),
            dma((6,)),
            dma((Z - 1,)),
            dma((Z - 1,)),
            dma((Z - 1,)),
            dma((Z - 1,)),
            dma,
            dma,
        ],
        compiler_params=pltpu.CompilerParams(
            collective_id=1, has_side_effects=True, vmem_limit_bytes=40 << 20
        ),
    )(parts, sums)


def scatter_kernel(slots_ref, v_ref, o_ref, s_ref, wide, sem, *accs):
    count = v_ref.shape[0]
    slots, width = o_ref.shape
    row = lax.axis_index("row")
    per_table = slots_ref.shape[1] // (2 * Z)
    own = per_table // (Y * X)

    def fetch(t):
        at = (t // 2) * per_table + row * own + (t % 2) * 128
        return pltpu.make_async_copy(
            slots_ref.at[:, pl.ds(pl.multiple_of(at, 128), 128)], s_ref.at[t], sem.at[t]
        )

    for t in range(count // 128):
        fetch(t).start()

    def clear(i, c):
        for acc in accs:
            acc[pl.ds(pl.multiple_of(i * 256, 256), 256), :] = jnp.zeros((256, width), f32)
        return c

    lax.fori_loop(0, slots // 256, clear, 0)
    wide[...] = v_ref[...].astype(f32)
    for t in range(count // 128):
        fetch(t).wait()

    def step(g, c):
        for i in range(0, 128, 2):
            row0 = wide[pl.ds(g * 128 + i, 1), :]
            row1 = wide[pl.ds(g * 128 + i + 1, 1), :]
            for which, acc in enumerate(accs):
                slot0 = s_ref[g, which, i]
                slot1 = s_ref[g, which, i + 1]
                old0 = acc[pl.ds(slot0, 1), :]
                old1 = acc[pl.ds(slot1, 1), :]
                new0 = old0 + row0
                new1 = jnp.where(slot0 == slot1, new0, old1) + row1
                acc[pl.ds(slot0, 1), :] = new0
                acc[pl.ds(slot1, 1), :] = new1
        return c

    lax.fori_loop(0, count // 128, step, 0)

    def finish(i, c):
        at = pl.ds(pl.multiple_of(i * 128, 128), 128)
        total = accs[0][at, :]
        for acc in accs[1:]:
            total = total + acc[at, :]
        o_ref[at, :] = total.astype(o_ref.dtype)
        return c

    lax.fori_loop(0, slots // 128, finish, 0)


def scatter_rows(slots, values, total_slots):
    count, width = values.shape
    hot = slots.shape[0]
    return pl.pallas_call(
        scatter_kernel,
        out_shape=jax.ShapeDtypeStruct((total_slots, width), bf16),
        in_specs=[pl.BlockSpec(memory_space=pl.ANY), pl.BlockSpec(memory_space=pltpu.VMEM)],
        out_specs=pl.BlockSpec(memory_space=pltpu.VMEM),
        scratch_shapes=[
            pltpu.SMEM((count // 128, hot, 128), jnp.int32),
            pltpu.VMEM((count, width), f32),
            pltpu.SemaphoreType.DMA((count // 128,)),
        ]
        + [pltpu.VMEM((total_slots, width), f32)] * hot,
        compiler_params=pltpu.CompilerParams(vmem_limit_bytes=44 << 20),
        cost_estimate=pl.CostEstimate(
            flops=10_000_000, bytes_accessed=100_000_000, transcendentals=0
        ),
    )(slots, values)


def local(
    dense_feat,
    pooled,
    labels,
    cross_down,
    cross_up,
    cross_bias,
    w_hidden1,
    bias1,
    w_hidden2,
    bias2,
    w_logit,
    lookup_slots,
):
    width = dense_feat.shape[1]
    n_row = lax.axis_size("row")
    u_shard = 1024
    big = (dense_feat, pooled, cross_down, cross_up, w_hidden1, w_hidden2)
    rows = [one[None, :] for one in (labels, cross_bias, bias1, bias2, w_logit)]
    received, sums = dense_part(big, rows)
    partial = scatter_rows(
        jnp.transpose(lookup_slots[0]), received.reshape(-1, width), n_row * u_shard
    )
    row_grads, g_h1, g_h2, g_up, g_down, vecs = exchange(
        partial.reshape(n_row, u_shard, width), sums
    )
    return (
        row_grads[None],
        g_down,
        g_up,
        vecs[0, 0:136],
        g_h1,
        vecs[1, 0:64],
        g_h2,
        vecs[2, 0:64],
        vecs[3, 0:64],
    )


def solution(mesh):
    in_specs = (
        P(("table", "row"), None),
        P(("table", "row"), None),
        P(("table", "row")),
        P(),
        P(),
        P(),
        P(),
        P(),
        P(),
        P(),
        P(),
        P("table", None, None),
    )
    out_specs = (
        P("table", "row", None),
        P("row", None),
        P("row", None),
        P("row"),
        P("row", None),
        P("row"),
        P("row", None),
        P("row"),
        P("row"),
    )
    return jax.shard_map(local, mesh=mesh, in_specs=in_specs, out_specs=out_specs, check_vma=False)
```

```python
import jax
import jax.numpy as jnp
from jax import lax
from jax.experimental import pallas as pl
from jax.experimental.pallas import tpu as pltpu
from jax.sharding import PartitionSpec as P

loss_scale = 16.0


MESH = pl.DeviceIdType.MESH
X, Y, Z = 4, 4, 8
PIECE = 144
WIDE = 1024
f32, bf16 = jnp.float32, jnp.bfloat16


def place():
    table = lax.axis_index("table")
    row = lax.axis_index("row")
    core, z = lax.rem(table, 2), table // 2
    y, x = row // X, lax.rem(row, X)
    return table, row, core, z, y, x


def slot_of(half, shard, y, x):
    dy = lax.rem(shard // X - y + Y, Y)
    dx = lax.rem(lax.rem(shard, X) - x + X, X)
    return dx * 4 + dy if half == 0 else dy * 4 + dx


def shard_of(core, y, x, first, second):
    dx = first * (1 - core) + second * core
    dy = second * (1 - core) + first * core
    return lax.rem(y + dy, Y) * X + lax.rem(x + dx, X)


def transposed(dst, src):
    for i in range(src.shape[1] // 128):
        at = slice(128 * i, 128 * i + 128)
        dst[at, :] = src[:, at].T


def ring(chunk, cut, size, vias, accs, gots, send, recv, plus, minus):
    low, high = pl.ds(0, cut), pl.ds(cut, size - cut)
    pairs = (
        (lambda: chunk(2).at[low], vias[0], plus),
        (lambda: chunk(2).at[high], vias[1], minus),
        (lambda: chunk(1).at[high], gots[0].at[high], plus),
        (lambda: chunk(3).at[low], gots[1].at[low], minus),
        (lambda: accs[0], gots[0].at[low], plus),
        (lambda: accs[1], gots[1].at[high], minus),
    )

    def copy(k):
        src, dst, who = pairs[k]
        return remote(src(), dst, send.at[k], recv.at[k], who)

    return copy


def remote(src, dst, s, r, who):
    return pltpu.make_async_remote_copy(
        src_ref=src, dst_ref=dst, send_sem=s, recv_sem=r, device_id=who, device_id_type=MESH
    )


def go(copies, *which):
    for k in which:
        copies(k).start()


def arrived(copies, *which):
    for k in which:
        copies(k).wait_recv()


def dot(a, b):
    return jnp.dot(a, b, preferred_element_type=f32)


def dot_t(a, b):
    return lax.dot_general(a, b, (((1,), (1,)), ((), ())), preferred_element_type=f32)


def tiles(body, width):
    for i in range(width // 256):
        body(slice(256 * i, 256 * i + 256), i)
    if width % 256:
        body(slice(width - width % 256, width), width // 256)


def dense_kernel(
    dense_feat,
    pooled,
    cross_down,
    cross_up,
    w_hidden1,
    w_hidden2,
    labels,
    cross_bias,
    bias1,
    bias2,
    w_logit,
    received,
    out,
    stacked,
    down_w,
    up_w,
    w1,
    w2,
    wide_plus,
    crossed,
    slope1,
    slope2,
    act_first,
    act_second,
    delta_second,
    delta_first,
    delta_crossed,
    delta_widened,
    reduced,
    delta_reduced,
    grad_logit,
    ready,
    packed,
    landed,
    flipped,
    small,
    via_plus,
    via_minus,
    got_plus,
    got_minus,
    load_sem,
    tsend,
    trecv,
    send_sem,
    recv_sem,
    send1,
    recv1,
    own_sem,
):
    table, row, core, z, y, x = place()
    n_table = 2 * Z
    other = z * 2 + 1 - core

    loads = [
        pltpu.make_async_copy(dense_feat, stacked.at[:, pl.ds(0, 128)], load_sem.at[0]),
        pltpu.make_async_copy(pooled, stacked.at[:, pl.ds(128, 2048)], load_sem.at[1]),
        pltpu.make_async_copy(cross_down, down_w, load_sem.at[2]),
        pltpu.make_async_copy(cross_up, up_w, load_sem.at[3]),
    ]
    for k in range(4):
        part = pl.ds(544 * k, 544)
        loads.append(pltpu.make_async_copy(w_hidden1.at[part], w1.at[part], load_sem.at[4 + k]))
    for k in range(2):
        part = pl.ds(512 * k, 512)
        loads.append(pltpu.make_async_copy(w_hidden2.at[part], w2.at[part], load_sem.at[8 + k]))
    for one in loads:
        one.start()

    def first_peer(d):
        return (table, shard_of(core, y, x, d, 0))

    barrier = pltpu.get_barrier_semaphore()
    for d in range(1, n_table):
        who = (lax.rem(table + d, n_table), row)
        pl.semaphore_signal(barrier, inc=1, device_id=who, device_id_type=MESH)
    for d in (1, 3):
        pl.semaphore_signal(barrier, inc=1, device_id=first_peer(d), device_id_type=MESH)

    def exchange_table(d):
        to = lax.rem(table + d, n_table)
        return remote(
            ready.at[to + 1], received.at[table], tsend.at[d - 1], trecv.at[d - 1], (to, row)
        )

    def came_table(d):
        came = lax.rem(table - d + n_table, n_table)
        return remote(
            ready.at[came + 1], received.at[came], tsend.at[d - 1], trecv.at[d - 1], (came, row)
        )

    def own_table():
        return pltpu.make_async_copy(ready.at[table + 1], received.at[table], own_sem)

    for k in (0, 1, 2):
        loads[k].wait()
    reduced[...] = dot(stacked[...], down_w[...]).astype(bf16)
    loads[3].wait()

    def cross(at, i):
        widened = dot(reduced[...], up_w[:, at]) + cross_bias[at][None, :]
        base = stacked[:, at].astype(f32)
        crossed[:, at] = (base * widened + base).astype(bf16)
        wide_plus[:, at] = widened + 1.0

    tiles(cross, 2176)
    for k in range(4, 8):
        loads[k].wait()

    def first_layer(at, i):
        pre = dot(crossed[...], w1[:, at]) + bias1[:, at]
        sig = jax.nn.sigmoid(pre)
        act_first[:, at] = (pre * sig).astype(bf16)
        slope1[:, at] = sig * (1.0 + pre * (1.0 - sig))

    tiles(first_layer, 1024)
    for k in range(8, 10):
        loads[k].wait()

    def second_layer(at, logits):
        pre = dot(act_first[...], w2[:, at]) + bias2[:, at]
        sig = jax.nn.sigmoid(pre)
        act = (pre * sig).astype(bf16)
        act_second[:, at] = act
        slope2[:, at] = sig * (1.0 + pre * (1.0 - sig))
        return logits + jnp.sum(act.astype(f32) * w_logit[:, at], axis=1, keepdims=True)

    logits = jnp.zeros((256, 1), f32)
    for i in range(1024 // 256):
        logits = second_layer(slice(256 * i, 256 * i + 256), logits)
    same = lax.broadcasted_iota(jnp.int32, (256, 256), 0) == lax.broadcasted_iota(
        jnp.int32, (256, 256), 1
    )
    label = jnp.sum(jnp.where(same, labels[...].astype(f32), 0.0), axis=1, keepdims=True)
    delta_logit = loss_scale * (jax.nn.sigmoid(logits) - label)

    def back_second(at, i):
        delta_second[:, at] = (delta_logit * w_logit[:, at] * slope2[:, at]).astype(bf16)
        grad_logit[:, at] = jnp.sum(
            act_second[:, at].astype(f32) * delta_logit, axis=0, keepdims=True
        )

    tiles(back_second, 1024)

    def back_first(at, i):
        back = dot_t(delta_second[...], w2[at, :])
        delta_first[:, at] = (back * slope1[:, at]).astype(bf16)

    tiles(back_first, 1024)

    def back_cross(at, i):
        delta = dot_t(delta_first[...], w1[at, :])
        delta_crossed[:, at] = delta
        delta_widened[:, at] = (delta * stacked[:, at].astype(f32)).astype(bf16)

    tiles(back_cross, 2176)
    delta_reduced[...] = dot_t(delta_widened[...], up_w[...]).astype(bf16)

    def back_stacked(at, i):
        delta = delta_crossed[:, at] * wide_plus[:, at] + dot_t(delta_reduced[...], down_w[at, :])
        for k in range(delta.shape[1] // 128):
            ready[2 * i + k] = delta[:, 128 * k : 128 * k + 128].astype(bf16)

    tiles(back_stacked, 2176)
    pl.semaphore_wait(barrier, n_table + 1)
    for d in range(1, n_table):
        exchange_table(d).start()
    own_table().start()

    def copy(half, slot):
        return remote(
            packed.at[half, slot], landed.at[slot], send_sem.at[slot], recv_sem.at[slot], (other, row)
        )

    transposed(flipped, act_first)

    def second(i, c):
        m = dot(flipped[slice(256 * i, 256 * i + 256), :], delta_second[...])
        for k in range(4):
            packed[1, slot_of(1, i * 4 + k, y, x), 0:64, :] = m[64 * k : 64 * k + 64].astype(bf16)
        return c

    for i in range(4):
        second(i, 0)

    transposed(small, reduced)

    def up(i, c):
        left = small[slice(64 * i, 64 * i + 64), :]
        m0 = dot(left, delta_widened[:, 0:1024])
        m1 = dot(left, delta_widened[:, 1024:2048])
        m2 = dot(left, delta_widened[:, 2048:2176])
        for k in range(4):
            slot = slot_of(1, i * 4 + k, y, x)
            part = slice(16 * k, 16 * k + 16)
            packed[1, slot, 64:80, :] = m0[part].astype(bf16)
            packed[1, slot, 80:96, :] = m1[part].astype(bf16)
            packed[1, slot, 96:112, 768:896] = m2[part].astype(bf16)
            packed[1, slot, 96:112, 896:1024] = jnp.zeros((16, 128), bf16)
            packed[1, slot, 128:144, 768:1024] = jnp.zeros((16, 256), bf16)
        return c

    for i in range(4):
        up(i, 0)

    transposed(flipped, stacked)

    def down(i, c):
        m = dot(flipped[slice(272 * i, 272 * i + 272), :], delta_reduced[...])
        for k in range(2):
            slot = slot_of(1, i * 2 + k, y, x)
            d = m[136 * k : 136 * k + 136]
            packed[1, slot, 96:144, 0:256] = d[0:48].astype(bf16)
            packed[1, slot, 96:144, 256:512] = d[48:96].astype(bf16)
            last = jnp.concatenate([d[96:136], jnp.zeros((8, 256), f32)], axis=0)
            packed[1, slot, 96:144, 512:768] = last.astype(bf16)
        return c

    for i in range(8):
        down(i, 0)

    ones = jnp.ones((8, 256), bf16)
    wide_sums = dot(ones, delta_widened[...])
    which = lax.broadcasted_iota(jnp.int32, (8, 1024), 0)
    sums = jnp.where(which == 1, dot(ones, delta_first[...]), dot(ones, delta_second[...]))
    sums = jnp.where(which == 3, grad_logit[...], sums)
    first_row = which[:, 0:256] == 0
    for shard in range(16):
        a = wide_sums if shard == 0 else pltpu.roll(wide_sums, 2176 - 136 * shard, 1)
        b = sums if shard == 0 else pltpu.roll(sums, 1024 - 64 * shard, 1)
        block = jnp.where(first_row, a[:, 0:256], b[:, 0:256])
        block = jnp.concatenate([block, jnp.zeros((8, 256), f32)], axis=0).astype(bf16)
        packed[1, slot_of(1, shard, y, x), 112:128, 768:1024] = block

    order = (8, 9, 10, 11, 4, 12, 5, 13, 6, 14, 7, 15, 0, 1, 2, 3)

    @pl.when(core == 0)
    def _():
        for slot in order:
            copy(1, slot).start()

    transposed(flipped, crossed)

    def first(i, c):
        m = dot(flipped[slice(272 * i, 272 * i + 272), :], delta_first[...])
        for k in range(2):
            slot = slot_of(0, i * 2 + k, y, x)
            d = jnp.concatenate([m[136 * k : 136 * k + 136], jnp.zeros((8, WIDE), f32)], axis=0)
            packed[0, slot] = d.astype(bf16)
        return c

    for i in range(8):
        first(i, 0)

    @pl.when(core == 1)
    def _():
        for slot in order:
            copy(0, slot).start()

    cut = 80

    def ring1(j):
        return ring(
            lambda d: packed.at[core, d * 4 + j],
            cut,
            PIECE,
            (via_plus.at[j], via_minus.at[j]),
            (packed.at[core, 4 + j, pl.ds(0, cut)], packed.at[core, 12 + j, pl.ds(cut, PIECE - cut)]),
            (got_plus.at[j], got_minus.at[j]),
            send1.at[j],
            recv1.at[j],
            first_peer(1),
            first_peer(3),
        )

    def add_pair(slot):
        copy(1 - core, slot).wait_recv()
        packed[core, slot] = (packed[core, slot].astype(f32) + landed[slot].astype(f32)).astype(bf16)

    def go_far(j, c):
        add_pair(8 + j)
        go(ring1(j), 0, 1)
        return c

    lax.fori_loop(0, 4, go_far, 0)

    def go_near(j, c):
        add_pair(4 + j)
        go(ring1(j), 2)
        add_pair(12 + j)
        go(ring1(j), 3)
        return c

    lax.fori_loop(0, 4, go_near, 0)

    def go_on(j, c):
        arrived(ring1(j), 0, 1)
        low, high = pl.ds(0, cut), pl.ds(cut, PIECE - cut)
        packed[core, 4 + j, low] = (
            packed[core, 4 + j, low].astype(f32) + via_plus[j].astype(f32)
        ).astype(bf16)
        packed[core, 12 + j, high] = (
            packed[core, 12 + j, high].astype(f32) + via_minus[j].astype(f32)
        ).astype(bf16)
        go(ring1(j), 4, 5)
        return c

    lax.fori_loop(0, 4, go_on, 0)

    def keep(j, c):
        add_pair(j)
        return c

    lax.fori_loop(0, 4, keep, 0)

    def finish(j, c):
        arrived(ring1(j), 2, 3, 4, 5)
        total = packed[core, j].astype(f32) + got_plus[j].astype(f32) + got_minus[j].astype(f32)
        out[j] = total.astype(bf16)
        return c

    lax.fori_loop(0, 4, finish, 0)

    def drain(slot, c):
        copy(1 - core, slot).wait_send()
        return c

    lax.fori_loop(0, 16, drain, 0)

    def drain1(j, c):
        for k in range(6):
            ring1(j)(k).wait_send()
        return c

    lax.fori_loop(0, 4, drain1, 0)
    own_table().wait()
    for d in range(1, n_table):
        came_table(d).wait_recv()
        exchange_table(d).wait_send()


def dense_part(big, rows):
    vmem = pl.BlockSpec(memory_space=pltpu.VMEM)
    anywhere = pl.BlockSpec(memory_space=pl.ANY)
    n_table = 2 * Z
    dma = pltpu.SemaphoreType.DMA
    return pl.pallas_call(
        dense_kernel,
        out_shape=(
            jax.ShapeDtypeStruct((n_table, 256, 128), bf16),
            jax.ShapeDtypeStruct((4, PIECE, WIDE), bf16),
        ),
        in_specs=[anywhere] * 6 + [vmem] * 5,
        out_specs=(anywhere, vmem),
        scratch_shapes=[
            pltpu.VMEM((256, 2176), bf16),
            pltpu.VMEM((2176, 256), bf16),
            pltpu.VMEM((256, 2176), bf16),
            pltpu.VMEM((2176, 1024), bf16),
            pltpu.VMEM((1024, 1024), bf16),
            pltpu.VMEM((256, 2176), f32),
            pltpu.VMEM((256, 2176), bf16),
            pltpu.VMEM((256, 1024), f32),
            pltpu.VMEM((256, 1024), f32),
            pltpu.VMEM((256, 1024), bf16),
            pltpu.VMEM((256, 1024), bf16),
            pltpu.VMEM((256, 1024), bf16),
            pltpu.VMEM((256, 1024), bf16),
            pltpu.VMEM((256, 2176), f32),
            pltpu.VMEM((256, 2176), bf16),
            pltpu.VMEM((256, 256), bf16),
            pltpu.VMEM((256, 256), bf16),
            pltpu.VMEM((1, 1024), f32),
            pltpu.VMEM((n_table + 1, 256, 128), bf16),
            pltpu.VMEM((2, 16, PIECE, WIDE), bf16),
            pltpu.VMEM((16, PIECE, WIDE), bf16),
            pltpu.VMEM((2176, 256), bf16),
            pltpu.VMEM((256, 256), bf16),
            pltpu.VMEM((4, 80, WIDE), bf16),
            pltpu.VMEM((4, 64, WIDE), bf16),
            pltpu.VMEM((4, PIECE, WIDE), bf16),
            pltpu.VMEM((4, PIECE, WIDE), bf16),
            dma((10,)),
            dma((n_table - 1,)),
            dma((n_table - 1,)),
            dma((16,)),
            dma((16,)),
            dma((4, 6)),
            dma((4, 6)),
            dma,
        ],
        compiler_params=pltpu.CompilerParams(
            collective_id=0, has_side_effects=True, vmem_limit_bytes=58 << 20
        ),
    )(*big, *rows)


def blocks(count, size, body):
    for i in range(count):
        body(slice(i * size, i * size + size))


def exchange_kernel(
    parts,
    dense_mid,
    row_out,
    final,
    via_plus,
    via_minus,
    acc_plus,
    acc_minus,
    got_plus,
    got_minus,
    mid,
    via2,
    got2,
    dense_via_plus,
    dense_via_minus,
    dense_acc_plus,
    dense_acc_minus,
    dense_got,
    zparts,
    zgot,
    own,
    own_sem,
    send1,
    recv1,
    send2,
    recv2,
    wsend,
    wrecv,
    zsend,
    zrecv,
    gsend,
    grecv,
    csend,
    crecv,
):
    table, row, core, z, y, x = place()
    sibling = z * 2 + 1 - core
    rows = parts.shape[1]

    def first_peer(d):
        return (table, shard_of(core, y, x, d, 0))

    def second_peer(j):
        return (table, shard_of(core, y, x, 0, j))

    def z_peer(d):
        return (lax.rem(z + d, Z) * 2 + core, row)

    barrier = pltpu.get_barrier_semaphore()
    peers = [first_peer(1), first_peer(3), second_peer(1), second_peer(3)]
    peers += [z_peer(d) for d in range(1, Z)] + [(sibling, row)]
    for who in peers:
        pl.semaphore_signal(barrier, inc=1, device_id=who, device_id_type=MESH)
    pl.semaphore_wait(barrier, len(peers))

    half = rows // 2

    def ring1(j):
        return ring(
            lambda d: parts.at[shard_of(core, y, x, d, j)],
            half,
            rows,
            (via_plus.at[j], via_minus.at[j]),
            (acc_plus.at[j], acc_minus.at[j]),
            (got_plus.at[j], got_minus.at[j]),
            send1.at[j],
            recv1.at[j],
            first_peer(1),
            first_peer(3),
        )

    def ring2():
        return ring(
            lambda d: mid.at[d],
            half,
            rows,
            (via2.at[0], via2.at[1]),
            (mid.at[1, pl.ds(0, half)], mid.at[3, pl.ds(half, half)]),
            (got2.at[0], got2.at[1]),
            send2,
            recv2,
            second_peer(1),
            second_peer(3),
        )

    cut = 80

    def ringw():
        return ring(
            lambda d: dense_mid.at[d],
            cut,
            PIECE,
            (dense_via_plus, dense_via_minus),
            (dense_acc_plus, dense_acc_minus),
            (dense_got.at[0], dense_got.at[1]),
            wsend,
            wrecv,
            second_peer(1),
            second_peer(3),
        )

    def copyz(d):
        return remote(
            zparts.at[lax.rem(z + d, Z)], zgot.at[d - 1], zsend.at[d - 1], zrecv.at[d - 1], z_peer(d)
        )

    def copyg(d, which):
        piece = final.at[core, which]
        return remote(piece, piece, gsend.at[d - 1], grecv.at[d - 1], z_peer(d))

    def copyc(half):
        return remote(final.at[half], final.at[half], csend, crecv, (sibling, row))

    def add_up(*terms):
        total = terms[0].astype(f32)
        for term in terms[1:]:
            total = total + term.astype(f32)
        return total

    def local(k, j):
        src, dst = (
            (parts.at[shard_of(core, y, x, 1, j), pl.ds(0, half)], acc_plus.at[j]),
            (parts.at[shard_of(core, y, x, 3, j), pl.ds(half, half)], acc_minus.at[j]),
            (parts.at[shard_of(core, y, x, 0, j)], own.at[j]),
        )[k]
        return pltpu.make_async_copy(src, dst, own_sem.at[k, j])

    def forward(j):
        copies = ring1(j)
        local(0, j).wait()
        arrived(copies, 0)

        def plus(at):
            acc_plus[j, at, :] = add_up(acc_plus[j, at, :], via_plus[j, at, :]).astype(bf16)

        blocks(half // 128, 128, plus)
        go(copies, 4)
        local(1, j).wait()
        arrived(copies, 1)

        def minus(at):
            acc_minus[j, at, :] = add_up(acc_minus[j, at, :], via_minus[j, at, :]).astype(bf16)

        blocks(half // 128, 128, minus)
        go(copies, 5)

    def row_mid(j):
        local(2, j).wait()
        arrived(ring1(j), 2, 3, 4, 5)

        def block(at):
            total = add_up(own[j, at, :], got_plus[j, at, :], got_minus[j, at, :])
            mid[j, at, :] = total.astype(bf16)

        blocks(rows // 128, 128, block)

    go(ringw(), 0, 1)
    go(ring1(2), 0, 1)
    go(ringw(), 2, 3)
    go(ring1(2), 2, 3)
    go(ring1(1), 0, 1)
    for j in (2, 1, 3, 0):
        for k in range(3):
            local(k, j).start()
    arrived(ringw(), 0, 1)

    def dense_plus(at):
        dense_acc_plus[at, :] = add_up(dense_mid[1, at, :], dense_via_plus[at, :]).astype(bf16)

    def dense_minus(at):
        later = slice(cut + at.start, cut + at.stop)
        dense_acc_minus[at, :] = add_up(dense_mid[3, later, :], dense_via_minus[at, :]).astype(bf16)

    blocks(cut // 16, 16, dense_plus)
    blocks((PIECE - cut) // 16, 16, dense_minus)
    go(ringw(), 4, 5)
    forward(2)
    go(ring1(1), 2, 3)
    go(ring1(3), 0, 1)
    forward(1)
    go(ring1(3), 2, 3)
    go(ring1(0), 0, 1)
    arrived(ringw(), 2, 3, 4, 5)

    def dense_last(at):
        total = add_up(dense_mid[0, at, :], dense_got[0, at, :], dense_got[1, at, :]).astype(bf16)
        for k in range(Z):
            zparts[k, at, :] = total[:, 128 * k : 128 * k + 128]

    blocks(PIECE // 16, 16, dense_last)
    for d in range(1, Z):
        copyz(d).start()
    forward(3)
    go(ring1(0), 2, 3)
    for d in range(1, Z):
        copyz(d).wait_recv()
    final[core, z] = add_up(zparts[z], *[zgot[d - 1] for d in range(1, Z)]).astype(bf16)
    for d in range(1, Z):
        copyg(d, z).start()
    row_mid(2)
    go(ring2(), 0, 1)
    forward(0)
    row_mid(1)
    go(ring2(), 2)
    for d in range(1, Z):
        copyg(d, lax.rem(z - d + Z, Z)).wait_recv()
    copyc(core).start()
    row_mid(3)
    go(ring2(), 3)
    arrived(ring2(), 0, 1)

    def mid_add(at):
        later = slice(half + at.start, half + at.stop)
        mid[1, at, :] = add_up(mid[1, at, :], via2[0, at, :]).astype(bf16)
        mid[3, later, :] = add_up(mid[3, later, :], via2[1, at, :]).astype(bf16)

    blocks(half // 128, 128, mid_add)
    go(ring2(), 4, 5)
    copyc(1 - core).wait_recv()
    arrived(ring1(0), 2, 3, 4, 5)
    arrived(ring2(), 2, 3, 4, 5)

    local(2, 0).wait()

    def row_last(at):
        row_out[at, :] = add_up(
            own[0, at, :],
            got_plus[0, at, :],
            got_minus[0, at, :],
            got2[0, at, :],
            got2[1, at, :],
        )

    blocks(rows // 128, 128, row_last)

    for j in range(4):
        for k in range(6):
            ring1(j)(k).wait_send()
    for k in range(6):
        ring2()(k).wait_send()
        ringw()(k).wait_send()
    for d in range(1, Z):
        copyz(d).wait_send()
        copyg(d, z).wait_send()
    copyc(core).wait_send()


def unpack_kernel(
    final,
    rows,
    row_out,
    down_out,
    up_out,
    cross_bias_out,
    h1_out,
    bias1_out,
    h2_out,
    bias2_out,
    logit_out,
):
    row_out[0] = rows[...]
    for k in range(Z):
        at = slice(128 * k, 128 * k + 128)
        h1_out[:, at] = final[0, k, :, :].astype(f32)[0:136]
        h2_out[:, at] = final[1, k, 0:64, :].astype(f32)
        up_out[:, at] = final[1, k, 64:80, :].astype(f32)
        up_out[:, 1024 + 128 * k : 1024 + 128 * k + 128] = final[1, k, 80:96, :].astype(f32)
    up_out[:, 2048:2176] = final[1, 6, 96:112, :].astype(f32)
    for k in range(2):
        at = slice(128 * k, 128 * k + 128)
        down_out[0:48, at] = final[1, k, 96:144, :].astype(f32)
        down_out[48:96, at] = final[1, 2 + k, 96:144, :].astype(f32)
        down_out[96:136, at] = final[1, 4 + k, 96:144, :].astype(f32)[0:40]
    low = final[1, 6, 112:128, :].astype(f32)
    high = final[1, 7, 112:128, :].astype(f32)
    cross_bias_out[pl.ds(0, 128)] = low[0]
    cross_bias_out[pl.ds(128, 8)] = high[0, 0:8]
    for k, one in enumerate((bias1_out, bias2_out, logit_out)):
        one[...] = low[k + 1, 0:64]


def unpack(final, rows):
    vmem = pl.BlockSpec(memory_space=pltpu.VMEM)
    shapes = ((1,) + rows.shape, (136, 256), (16, 2176), (136,), (136, 1024), (64,), (64, 1024))
    shapes += ((64,), (64,))
    return pl.pallas_call(
        unpack_kernel,
        out_shape=tuple(jax.ShapeDtypeStruct(shape, f32) for shape in shapes),
        in_specs=[vmem] * 2,
        out_specs=(vmem,) * 9,
        compiler_params=pltpu.CompilerParams(vmem_limit_bytes=16 << 20),
    )(final, rows)


def exchange(parts, sums):
    vmem = pl.BlockSpec(memory_space=pltpu.VMEM)
    rows, width = parts.shape[1:]
    half = rows // 2
    dma = pltpu.SemaphoreType.DMA
    return pl.pallas_call(
        exchange_kernel,
        out_shape=(
            jax.ShapeDtypeStruct((rows, width), f32),
            jax.ShapeDtypeStruct((2, Z, PIECE, 128), bf16),
        ),
        in_specs=[pl.BlockSpec(memory_space=pl.ANY), vmem],
        out_specs=(vmem,) * 2,
        scratch_shapes=[
            pltpu.VMEM((4, half, width), bf16),
            pltpu.VMEM((4, half, width), bf16),
            pltpu.VMEM((4, half, width), bf16),
            pltpu.VMEM((4, half, width), bf16),
            pltpu.VMEM((4, rows, width), bf16),
            pltpu.VMEM((4, rows, width), bf16),
            pltpu.VMEM((4, rows, width), bf16),
            pltpu.VMEM((2, half, width), bf16),
            pltpu.VMEM((2, rows, width), bf16),
            pltpu.VMEM((80, WIDE), bf16),
            pltpu.VMEM((64, WIDE), bf16),
            pltpu.VMEM((80, WIDE), bf16),
            pltpu.VMEM((64, WIDE), bf16),
            pltpu.VMEM((2, PIECE, WIDE), bf16),
            pltpu.VMEM((Z, PIECE, 128), bf16),
            pltpu.VMEM((Z - 1, PIECE, 128), bf16),
            pltpu.VMEM((4, rows, width), bf16),
            dma((3, 4)),
            dma((4, 6)),
            dma((4, 6)),
            dma((6,)),
            dma((6,)),
            dma((6,)),
            dma((6,)),
            dma((Z - 1,)),
            dma((Z - 1,)),
            dma((Z - 1,)),
            dma((Z - 1,)),
            dma,
            dma,
        ],
        compiler_params=pltpu.CompilerParams(
            collective_id=1, has_side_effects=True, vmem_limit_bytes=61 << 20
        ),
    )(parts, sums)


def scatter_kernel(
    slots_ref, values_ref, o_ref, s_ref, narrow, wide, done, sem, value_sem, out_sem, *accs
):
    count, width = wide.shape
    slots = o_ref.shape[0]
    row = lax.axis_index("row")
    per_table = slots_ref.shape[1] // (2 * Z)
    own = per_table // (Y * X)
    values = pltpu.make_async_copy(values_ref, narrow, value_sem)
    values.start()

    def fetch(t):
        at = (t // 2) * per_table + row * own + (t % 2) * 128
        return pltpu.make_async_copy(
            slots_ref.at[:, pl.ds(pl.multiple_of(at, 128), 128)], s_ref.at[t], sem.at[t]
        )

    for t in range(count // 128):
        fetch(t).start()

    def clear(i, c):
        for acc in accs:
            acc[pl.ds(pl.multiple_of(i * 512, 512), 512), :] = jnp.zeros((512, width), f32)
        return c

    lax.fori_loop(0, slots // 512, clear, 0)
    values.wait()
    wide[...] = narrow[...].astype(f32)
    for t in range(count // 128):
        fetch(t).wait()

    def step(g, c):
        turn = 0
        for i in range(128):
            sample = wide[pl.ds(g * 128 + i, 1), :]
            for which in range(s_ref.shape[1]):
                acc = accs[turn % len(accs)]
                turn += 1
                at = pl.ds(s_ref[g, which, i], 1)
                acc[at, :] = acc[at, :] + sample
        return c

    lax.fori_loop(0, count // 128, step, 0)

    def leave(i):
        at = pl.ds(pl.multiple_of(i * 1024, 1024), 1024)
        return pltpu.make_async_copy(done.at[at], o_ref.at[at], out_sem.at[i])

    def finish(i, c):
        for part in range(2):
            at = pl.ds(pl.multiple_of(i * 1024 + part * 512, 512), 512)
            total = accs[0][at, :]
            for acc in accs[1:]:
                total = total + acc[at, :]
            done[at, :] = total.astype(bf16)
        leave(i).start()
        return c

    lax.fori_loop(0, slots // 1024, finish, 0)
    for i in range(slots // 1024):
        leave(i).wait()


def scatter_rows(slots, values, total_slots):
    count, width = values.shape
    hot = slots.shape[0]
    anywhere = pl.BlockSpec(memory_space=pl.ANY)
    return pl.pallas_call(
        scatter_kernel,
        out_shape=jax.ShapeDtypeStruct((total_slots, width), bf16),
        in_specs=[anywhere, anywhere],
        out_specs=anywhere,
        scratch_shapes=[
            pltpu.SMEM((count // 128, hot, 128), jnp.int32),
            pltpu.VMEM((count, width), bf16),
            pltpu.VMEM((count, width), f32),
            pltpu.VMEM((total_slots, width), bf16),
            pltpu.SemaphoreType.DMA((count // 128,)),
            pltpu.SemaphoreType.DMA,
            pltpu.SemaphoreType.DMA((total_slots // 1024,)),
        ]
        + [pltpu.VMEM((total_slots, width), f32)] * 6,
        compiler_params=pltpu.CompilerParams(vmem_limit_bytes=57 << 20),
        cost_estimate=pl.CostEstimate(
            flops=10_000_000, bytes_accessed=100_000_000, transcendentals=0
        ),
    )(slots, values)


def local(
    dense_feat,
    pooled,
    labels,
    cross_down,
    cross_up,
    cross_bias,
    w_hidden1,
    bias1,
    w_hidden2,
    bias2,
    w_logit,
    lookup_slots,
):
    width = dense_feat.shape[1]
    n_row = lax.axis_size("row")
    u_shard = 1024
    big = (dense_feat, pooled, cross_down, cross_up, w_hidden1, w_hidden2)
    rows = [labels[None, :], cross_bias, bias1[None, :], bias2[None, :], w_logit[None, :]]
    received, sums = dense_part(big, rows)
    partial = scatter_rows(
        jnp.transpose(lookup_slots[0]), received.reshape(-1, width), n_row * u_shard
    )
    row_sums, final = exchange(partial.reshape(n_row, u_shard, width), sums)
    return tuple(unpack(final, row_sums))


def solution(mesh):
    in_specs = (
        P(("table", "row"), None),
        P(("table", "row"), None),
        P(("table", "row")),
        P(),
        P(),
        P(),
        P(),
        P(),
        P(),
        P(),
        P(),
        P("table", None, None),
    )
    out_specs = (
        P("table", "row", None),
        P("row", None),
        P("row", None),
        P("row"),
        P("row", None),
        P("row"),
        P("row", None),
        P("row"),
        P("row"),
    )
    return jax.shard_map(local, mesh=mesh, in_specs=in_specs, out_specs=out_specs, check_vma=False)
```

```python
import jax
import jax.numpy as jnp
from jax import lax
from jax.experimental import pallas as pl
from jax.experimental.pallas import tpu as pltpu
from jax.sharding import PartitionSpec as P

loss_scale = 16.0


MESH = pl.DeviceIdType.MESH
X, Y, Z = 4, 4, 8
PIECE = 144
WIDE = 1024
f32, bf16 = jnp.float32, jnp.bfloat16


def place():
    table = lax.axis_index("table")
    row = lax.axis_index("row")
    core, z = lax.rem(table, 2), table // 2
    y, x = row // X, lax.rem(row, X)
    return table, row, core, z, y, x


def slot_of(half, shard, y, x):
    dy = lax.rem(shard // X - y + Y, Y)
    dx = lax.rem(lax.rem(shard, X) - x + X, X)
    return dx * 4 + dy if half == 0 else dy * 4 + dx


def shard_of(core, y, x, first, second):
    dx = first * (1 - core) + second * core
    dy = second * (1 - core) + first * core
    return lax.rem(y + dy, Y) * X + lax.rem(x + dx, X)


def transposed(dst, src):
    for i in range(src.shape[1] // 128):
        at = slice(128 * i, 128 * i + 128)
        dst[at, :] = src[:, at].T


def ring(chunk, cut, size, vias, accs, gots, send, recv, plus, minus):
    low, high = pl.ds(0, cut), pl.ds(cut, size - cut)
    pairs = (
        (lambda: chunk(2).at[low], vias[0], plus),
        (lambda: chunk(2).at[high], vias[1], minus),
        (lambda: chunk(1).at[high], gots[0].at[high], plus),
        (lambda: chunk(3).at[low], gots[1].at[low], minus),
        (lambda: accs[0], gots[0].at[low], plus),
        (lambda: accs[1], gots[1].at[high], minus),
    )

    def copy(k):
        src, dst, who = pairs[k]
        return remote(src(), dst, send.at[k], recv.at[k], who)

    return copy


def remote(src, dst, s, r, who):
    return pltpu.make_async_remote_copy(
        src_ref=src, dst_ref=dst, send_sem=s, recv_sem=r, device_id=who, device_id_type=MESH
    )


def go(copies, *which):
    for k in which:
        copies(k).start()


def arrived(copies, *which):
    for k in which:
        copies(k).wait_recv()


def dot(a, b):
    return jnp.dot(a, b, preferred_element_type=f32)


def dot_t(a, b):
    return lax.dot_general(a, b, (((1,), (1,)), ((), ())), preferred_element_type=f32)


def tiles(body, width):
    for i in range(width // 256):
        body(slice(256 * i, 256 * i + 256), i)
    if width % 256:
        body(slice(width - width % 256, width), width // 256)


def dense_kernel(
    dense_feat,
    pooled,
    cross_down,
    cross_up,
    w_hidden1,
    w_hidden2,
    labels,
    cross_bias,
    bias1,
    bias2,
    w_logit,
    received,
    out,
    stacked,
    down_w,
    up_w,
    w1,
    w2,
    wide_plus,
    crossed,
    slope1,
    slope2,
    act_first,
    act_second,
    delta_second,
    delta_first,
    delta_crossed,
    delta_widened,
    reduced,
    delta_reduced,
    grad_logit,
    ready,
    packed,
    landed,
    flipped,
    small,
    via_plus,
    via_minus,
    got_plus,
    got_minus,
    load_sem,
    tsend,
    trecv,
    send_sem,
    recv_sem,
    send1,
    recv1,
    own_sem,
):
    table, row, core, z, y, x = place()
    n_table = 2 * Z
    other = z * 2 + 1 - core

    loads = [
        pltpu.make_async_copy(dense_feat, stacked.at[:, pl.ds(0, 128)], load_sem.at[0]),
        pltpu.make_async_copy(pooled, stacked.at[:, pl.ds(128, 2048)], load_sem.at[1]),
        pltpu.make_async_copy(cross_down, down_w, load_sem.at[2]),
        pltpu.make_async_copy(cross_up, up_w, load_sem.at[3]),
    ]
    for k in range(4):
        part = pl.ds(544 * k, 544)
        loads.append(pltpu.make_async_copy(w_hidden1.at[part], w1.at[part], load_sem.at[4 + k]))
    for k in range(2):
        part = pl.ds(512 * k, 512)
        loads.append(pltpu.make_async_copy(w_hidden2.at[part], w2.at[part], load_sem.at[8 + k]))
    for one in loads:
        one.start()

    def first_peer(d):
        return (table, shard_of(core, y, x, d, 0))

    barrier = pltpu.get_barrier_semaphore()
    for d in range(1, n_table):
        who = (lax.rem(table + d, n_table), row)
        pl.semaphore_signal(barrier, inc=1, device_id=who, device_id_type=MESH)
    for d in (1, 3):
        pl.semaphore_signal(barrier, inc=1, device_id=first_peer(d), device_id_type=MESH)

    def exchange_table(d):
        to = lax.rem(table + d, n_table)
        return remote(
            ready.at[to + 1], received.at[table], tsend.at[d - 1], trecv.at[d - 1], (to, row)
        )

    def came_table(d):
        came = lax.rem(table - d + n_table, n_table)
        return remote(
            ready.at[came + 1], received.at[came], tsend.at[d - 1], trecv.at[d - 1], (came, row)
        )

    def own_table():
        return pltpu.make_async_copy(ready.at[table + 1], received.at[table], own_sem)

    for k in (0, 1, 2):
        loads[k].wait()
    reduced[...] = dot(stacked[...], down_w[...]).astype(bf16)
    loads[3].wait()

    def cross(at, i):
        widened = dot(reduced[...], up_w[:, at]) + cross_bias[at][None, :]
        base = stacked[:, at].astype(f32)
        crossed[:, at] = (base * widened + base).astype(bf16)
        wide_plus[:, at] = widened + 1.0

    tiles(cross, 2176)
    for k in range(4, 8):
        loads[k].wait()

    def first_layer(at, i):
        pre = dot(crossed[...], w1[:, at]) + bias1[:, at]
        sig = jax.nn.sigmoid(pre)
        act_first[:, at] = (pre * sig).astype(bf16)
        slope1[:, at] = sig * (1.0 + pre * (1.0 - sig))

    tiles(first_layer, 1024)
    for k in range(8, 10):
        loads[k].wait()

    def second_layer(at, logits):
        pre = dot(act_first[...], w2[:, at]) + bias2[:, at]
        sig = jax.nn.sigmoid(pre)
        act = (pre * sig).astype(bf16)
        act_second[:, at] = act
        slope2[:, at] = sig * (1.0 + pre * (1.0 - sig))
        return logits + jnp.sum(act.astype(f32) * w_logit[:, at], axis=1, keepdims=True)

    logits = jnp.zeros((256, 1), f32)
    for i in range(1024 // 256):
        logits = second_layer(slice(256 * i, 256 * i + 256), logits)
    same = lax.broadcasted_iota(jnp.int32, (256, 256), 0) == lax.broadcasted_iota(
        jnp.int32, (256, 256), 1
    )
    label = jnp.sum(jnp.where(same, labels[...].astype(f32), 0.0), axis=1, keepdims=True)
    delta_logit = loss_scale * (jax.nn.sigmoid(logits) - label)

    def back_second(at, i):
        delta_second[:, at] = (delta_logit * w_logit[:, at] * slope2[:, at]).astype(bf16)
        grad_logit[:, at] = jnp.sum(
            act_second[:, at].astype(f32) * delta_logit, axis=0, keepdims=True
        )

    tiles(back_second, 1024)

    def back_first(at, i):
        back = dot_t(delta_second[...], w2[at, :])
        delta_first[:, at] = (back * slope1[:, at]).astype(bf16)

    tiles(back_first, 1024)

    def back_cross(at, i):
        delta = dot_t(delta_first[...], w1[at, :])
        delta_crossed[:, at] = delta
        delta_widened[:, at] = (delta * stacked[:, at].astype(f32)).astype(bf16)

    tiles(back_cross, 2176)
    delta_reduced[...] = dot_t(delta_widened[...], up_w[...]).astype(bf16)

    def back_stacked(at, i):
        delta = delta_crossed[:, at] * wide_plus[:, at] + dot_t(delta_reduced[...], down_w[at, :])
        for k in range(delta.shape[1] // 128):
            ready[2 * i + k] = delta[:, 128 * k : 128 * k + 128].astype(bf16)

    tiles(back_stacked, 2176)
    pl.semaphore_wait(barrier, n_table + 1)
    for d in range(1, n_table):
        exchange_table(d).start()
    own_table().start()

    def copy(half, slot):
        return remote(
            packed.at[half, slot], landed.at[slot], send_sem.at[slot], recv_sem.at[slot], (other, row)
        )

    transposed(flipped, act_first)

    def second(i, c):
        m = dot(flipped[slice(256 * i, 256 * i + 256), :], delta_second[...])
        for k in range(4):
            packed[1, slot_of(1, i * 4 + k, y, x), 0:64, :] = m[64 * k : 64 * k + 64].astype(bf16)
        return c

    for i in range(4):
        second(i, 0)

    transposed(small, reduced)

    def up(i, c):
        left = small[slice(64 * i, 64 * i + 64), :]
        m0 = dot(left, delta_widened[:, 0:1024])
        m1 = dot(left, delta_widened[:, 1024:2048])
        m2 = dot(left, delta_widened[:, 2048:2176])
        for k in range(4):
            slot = slot_of(1, i * 4 + k, y, x)
            part = slice(16 * k, 16 * k + 16)
            packed[1, slot, 64:80, :] = m0[part].astype(bf16)
            packed[1, slot, 80:96, :] = m1[part].astype(bf16)
            packed[1, slot, 96:112, 768:896] = m2[part].astype(bf16)
            packed[1, slot, 96:112, 896:1024] = jnp.zeros((16, 128), bf16)
            packed[1, slot, 128:144, 768:1024] = jnp.zeros((16, 256), bf16)
        return c

    for i in range(4):
        up(i, 0)

    transposed(flipped, stacked)

    def down(i, c):
        m = dot(flipped[slice(272 * i, 272 * i + 272), :], delta_reduced[...])
        for k in range(2):
            slot = slot_of(1, i * 2 + k, y, x)
            d = m[136 * k : 136 * k + 136]
            packed[1, slot, 96:144, 0:256] = d[0:48].astype(bf16)
            packed[1, slot, 96:144, 256:512] = d[48:96].astype(bf16)
            last = jnp.concatenate([d[96:136], jnp.zeros((8, 256), f32)], axis=0)
            packed[1, slot, 96:144, 512:768] = last.astype(bf16)
        return c

    for i in range(8):
        down(i, 0)

    ones = jnp.ones((8, 256), bf16)
    wide_sums = dot(ones, delta_widened[...])
    which = lax.broadcasted_iota(jnp.int32, (8, 1024), 0)
    sums = jnp.where(which == 1, dot(ones, delta_first[...]), dot(ones, delta_second[...]))
    sums = jnp.where(which == 3, grad_logit[...], sums)
    first_row = which[:, 0:256] == 0
    for shard in range(16):
        a = wide_sums if shard == 0 else pltpu.roll(wide_sums, 2176 - 136 * shard, 1)
        b = sums if shard == 0 else pltpu.roll(sums, 1024 - 64 * shard, 1)
        block = jnp.where(first_row, a[:, 0:256], b[:, 0:256])
        block = jnp.concatenate([block, jnp.zeros((8, 256), f32)], axis=0).astype(bf16)
        packed[1, slot_of(1, shard, y, x), 112:128, 768:1024] = block

    order = (8, 9, 10, 11, 4, 12, 5, 13, 6, 14, 7, 15, 0, 1, 2, 3)

    @pl.when(core == 0)
    def _():
        for slot in order:
            copy(1, slot).start()

    transposed(flipped, crossed)

    def first(i, c):
        m = dot(flipped[slice(272 * i, 272 * i + 272), :], delta_first[...])
        for k in range(2):
            slot = slot_of(0, i * 2 + k, y, x)
            d = jnp.concatenate([m[136 * k : 136 * k + 136], jnp.zeros((8, WIDE), f32)], axis=0)
            packed[0, slot] = d.astype(bf16)
        return c

    for i in range(8):
        first(i, 0)

    @pl.when(core == 1)
    def _():
        for slot in order:
            copy(0, slot).start()

    cut = 80

    def ring1(j):
        return ring(
            lambda d: packed.at[core, d * 4 + j],
            cut,
            PIECE,
            (via_plus.at[j], via_minus.at[j]),
            (packed.at[core, 4 + j, pl.ds(0, cut)], packed.at[core, 12 + j, pl.ds(cut, PIECE - cut)]),
            (got_plus.at[j], got_minus.at[j]),
            send1.at[j],
            recv1.at[j],
            first_peer(1),
            first_peer(3),
        )

    def add_pair(slot):
        copy(1 - core, slot).wait_recv()
        packed[core, slot] = (packed[core, slot].astype(f32) + landed[slot].astype(f32)).astype(bf16)

    def go_far(j, c):
        add_pair(8 + j)
        go(ring1(j), 0, 1)
        return c

    lax.fori_loop(0, 4, go_far, 0)

    def go_near(j, c):
        add_pair(4 + j)
        go(ring1(j), 2)
        add_pair(12 + j)
        go(ring1(j), 3)
        return c

    lax.fori_loop(0, 4, go_near, 0)

    def go_on(j, c):
        arrived(ring1(j), 0, 1)
        low, high = pl.ds(0, cut), pl.ds(cut, PIECE - cut)
        packed[core, 4 + j, low] = (
            packed[core, 4 + j, low].astype(f32) + via_plus[j].astype(f32)
        ).astype(bf16)
        packed[core, 12 + j, high] = (
            packed[core, 12 + j, high].astype(f32) + via_minus[j].astype(f32)
        ).astype(bf16)
        go(ring1(j), 4, 5)
        return c

    lax.fori_loop(0, 4, go_on, 0)

    def keep(j, c):
        add_pair(j)
        return c

    lax.fori_loop(0, 4, keep, 0)

    def finish(j, c):
        arrived(ring1(j), 2, 3, 4, 5)
        total = packed[core, j].astype(f32) + got_plus[j].astype(f32) + got_minus[j].astype(f32)
        out[j] = total.astype(bf16)
        return c

    lax.fori_loop(0, 4, finish, 0)

    def drain(slot, c):
        copy(1 - core, slot).wait_send()
        return c

    lax.fori_loop(0, 16, drain, 0)

    def drain1(j, c):
        for k in range(6):
            ring1(j)(k).wait_send()
        return c

    lax.fori_loop(0, 4, drain1, 0)
    own_table().wait()
    for d in range(1, n_table):
        came_table(d).wait_recv()
        exchange_table(d).wait_send()


def dense_part(big, rows):
    vmem = pl.BlockSpec(memory_space=pltpu.VMEM)
    anywhere = pl.BlockSpec(memory_space=pl.ANY)
    n_table = 2 * Z
    dma = pltpu.SemaphoreType.DMA
    return pl.pallas_call(
        dense_kernel,
        out_shape=(
            jax.ShapeDtypeStruct((n_table, 256, 128), bf16),
            jax.ShapeDtypeStruct((4, PIECE, WIDE), bf16),
        ),
        in_specs=[anywhere] * 6 + [vmem] * 5,
        out_specs=(anywhere, vmem),
        scratch_shapes=[
            pltpu.VMEM((256, 2176), bf16),
            pltpu.VMEM((2176, 256), bf16),
            pltpu.VMEM((256, 2176), bf16),
            pltpu.VMEM((2176, 1024), bf16),
            pltpu.VMEM((1024, 1024), bf16),
            pltpu.VMEM((256, 2176), f32),
            pltpu.VMEM((256, 2176), bf16),
            pltpu.VMEM((256, 1024), f32),
            pltpu.VMEM((256, 1024), f32),
            pltpu.VMEM((256, 1024), bf16),
            pltpu.VMEM((256, 1024), bf16),
            pltpu.VMEM((256, 1024), bf16),
            pltpu.VMEM((256, 1024), bf16),
            pltpu.VMEM((256, 2176), f32),
            pltpu.VMEM((256, 2176), bf16),
            pltpu.VMEM((256, 256), bf16),
            pltpu.VMEM((256, 256), bf16),
            pltpu.VMEM((1, 1024), f32),
            pltpu.VMEM((n_table + 1, 256, 128), bf16),
            pltpu.VMEM((2, 16, PIECE, WIDE), bf16),
            pltpu.VMEM((16, PIECE, WIDE), bf16),
            pltpu.VMEM((2176, 256), bf16),
            pltpu.VMEM((256, 256), bf16),
            pltpu.VMEM((4, 80, WIDE), bf16),
            pltpu.VMEM((4, 64, WIDE), bf16),
            pltpu.VMEM((4, PIECE, WIDE), bf16),
            pltpu.VMEM((4, PIECE, WIDE), bf16),
            dma((10,)),
            dma((n_table - 1,)),
            dma((n_table - 1,)),
            dma((16,)),
            dma((16,)),
            dma((4, 6)),
            dma((4, 6)),
            dma,
        ],
        compiler_params=pltpu.CompilerParams(
            collective_id=0, has_side_effects=True, vmem_limit_bytes=58 << 20
        ),
    )(*big, *rows)


def blocks(count, size, body):
    for i in range(count):
        body(slice(i * size, i * size + size))


def exchange_kernel(
    parts,
    dense_mid,
    row_out,
    final,
    via_plus,
    via_minus,
    acc_plus,
    acc_minus,
    got_plus,
    got_minus,
    mid,
    via2,
    got2,
    dense_via_plus,
    dense_via_minus,
    dense_acc_plus,
    dense_acc_minus,
    dense_got,
    zparts,
    zgot,
    own,
    own_sem,
    send1,
    recv1,
    send2,
    recv2,
    wsend,
    wrecv,
    zsend,
    zrecv,
    gsend,
    grecv,
    csend,
    crecv,
):
    table, row, core, z, y, x = place()
    sibling = z * 2 + 1 - core
    rows = parts.shape[1]

    def first_peer(d):
        return (table, shard_of(core, y, x, d, 0))

    def second_peer(j):
        return (table, shard_of(core, y, x, 0, j))

    def z_peer(d):
        return (lax.rem(z + d, Z) * 2 + core, row)

    barrier = pltpu.get_barrier_semaphore()
    peers = [first_peer(1), first_peer(3), second_peer(1), second_peer(3)]
    peers += [z_peer(d) for d in range(1, Z)] + [(sibling, row)]
    for who in peers:
        pl.semaphore_signal(barrier, inc=1, device_id=who, device_id_type=MESH)
    pl.semaphore_wait(barrier, len(peers))

    half = rows // 2

    def ring1(j):
        return ring(
            lambda d: parts.at[shard_of(core, y, x, d, j)],
            half,
            rows,
            (via_plus.at[j], via_minus.at[j]),
            (acc_plus.at[j], acc_minus.at[j]),
            (got_plus.at[j], got_minus.at[j]),
            send1.at[j],
            recv1.at[j],
            first_peer(1),
            first_peer(3),
        )

    def ring2():
        return ring(
            lambda d: mid.at[d],
            half,
            rows,
            (via2.at[0], via2.at[1]),
            (mid.at[1, pl.ds(0, half)], mid.at[3, pl.ds(half, half)]),
            (got2.at[0], got2.at[1]),
            send2,
            recv2,
            second_peer(1),
            second_peer(3),
        )

    cut = 80

    def ringw():
        return ring(
            lambda d: dense_mid.at[d],
            cut,
            PIECE,
            (dense_via_plus, dense_via_minus),
            (dense_acc_plus, dense_acc_minus),
            (dense_got.at[0], dense_got.at[1]),
            wsend,
            wrecv,
            second_peer(1),
            second_peer(3),
        )

    def copyz(d):
        return remote(
            zparts.at[lax.rem(z + d, Z)], zgot.at[d - 1], zsend.at[d - 1], zrecv.at[d - 1], z_peer(d)
        )

    def copyg(d, which):
        piece = final.at[core, which]
        return remote(piece, piece, gsend.at[d - 1], grecv.at[d - 1], z_peer(d))

    def copyc(half):
        return remote(final.at[half], final.at[half], csend, crecv, (sibling, row))

    def add_up(*terms):
        total = terms[0].astype(f32)
        for term in terms[1:]:
            total = total + term.astype(f32)
        return total

    def local(k, j):
        src, dst = (
            (parts.at[shard_of(core, y, x, 1, j), pl.ds(0, half)], acc_plus.at[j]),
            (parts.at[shard_of(core, y, x, 3, j), pl.ds(half, half)], acc_minus.at[j]),
            (parts.at[shard_of(core, y, x, 0, j)], own.at[j]),
        )[k]
        return pltpu.make_async_copy(src, dst, own_sem.at[k, j])

    def forward(j):
        copies = ring1(j)
        local(0, j).wait()
        arrived(copies, 0)

        def plus(at):
            acc_plus[j, at, :] = add_up(acc_plus[j, at, :], via_plus[j, at, :]).astype(bf16)

        blocks(half // 128, 128, plus)
        go(copies, 4)
        local(1, j).wait()
        arrived(copies, 1)

        def minus(at):
            acc_minus[j, at, :] = add_up(acc_minus[j, at, :], via_minus[j, at, :]).astype(bf16)

        blocks(half // 128, 128, minus)
        go(copies, 5)

    def row_mid(j):
        local(2, j).wait()
        arrived(ring1(j), 2, 3, 4, 5)

        def block(at):
            total = add_up(own[j, at, :], got_plus[j, at, :], got_minus[j, at, :])
            mid[j, at, :] = total.astype(bf16)

        blocks(rows // 128, 128, block)

    go(ringw(), 0, 1)
    go(ring1(2), 0, 1)
    go(ringw(), 2, 3)
    go(ring1(2), 2, 3)
    go(ring1(1), 0, 1)
    for j in (2, 1, 3, 0):
        for k in range(3):
            local(k, j).start()
    arrived(ringw(), 0, 1)

    def dense_plus(at):
        dense_acc_plus[at, :] = add_up(dense_mid[1, at, :], dense_via_plus[at, :]).astype(bf16)

    def dense_minus(at):
        later = slice(cut + at.start, cut + at.stop)
        dense_acc_minus[at, :] = add_up(dense_mid[3, later, :], dense_via_minus[at, :]).astype(bf16)

    blocks(cut // 16, 16, dense_plus)
    blocks((PIECE - cut) // 16, 16, dense_minus)
    go(ringw(), 4, 5)
    forward(2)
    go(ring1(1), 2, 3)
    go(ring1(3), 0, 1)
    forward(1)
    go(ring1(3), 2, 3)
    go(ring1(0), 0, 1)
    arrived(ringw(), 2, 3, 4, 5)

    def dense_last(at):
        total = add_up(dense_mid[0, at, :], dense_got[0, at, :], dense_got[1, at, :]).astype(bf16)
        for k in range(Z):
            zparts[k, at, :] = total[:, 128 * k : 128 * k + 128]

    blocks(PIECE // 16, 16, dense_last)
    for d in range(1, Z):
        copyz(d).start()
    forward(3)
    go(ring1(0), 2, 3)
    for d in range(1, Z):
        copyz(d).wait_recv()
    final[core, z] = add_up(zparts[z], *[zgot[d - 1] for d in range(1, Z)]).astype(bf16)
    for d in range(1, Z):
        copyg(d, z).start()
    row_mid(2)
    go(ring2(), 0, 1)
    forward(0)
    row_mid(1)
    go(ring2(), 2)
    for d in range(1, Z):
        copyg(d, lax.rem(z - d + Z, Z)).wait_recv()
    copyc(core).start()
    row_mid(3)
    go(ring2(), 3)
    arrived(ring2(), 0, 1)

    def mid_add(at):
        later = slice(half + at.start, half + at.stop)
        mid[1, at, :] = add_up(mid[1, at, :], via2[0, at, :]).astype(bf16)
        mid[3, later, :] = add_up(mid[3, later, :], via2[1, at, :]).astype(bf16)

    blocks(half // 128, 128, mid_add)
    go(ring2(), 4, 5)
    copyc(1 - core).wait_recv()
    arrived(ring1(0), 2, 3, 4, 5)
    arrived(ring2(), 2, 3, 4, 5)

    local(2, 0).wait()

    def row_last(at):
        row_out[at, :] = add_up(
            own[0, at, :],
            got_plus[0, at, :],
            got_minus[0, at, :],
            got2[0, at, :],
            got2[1, at, :],
        )

    blocks(rows // 128, 128, row_last)

    for j in range(4):
        for k in range(6):
            ring1(j)(k).wait_send()
    for k in range(6):
        ring2()(k).wait_send()
        ringw()(k).wait_send()
    for d in range(1, Z):
        copyz(d).wait_send()
        copyg(d, z).wait_send()
    copyc(core).wait_send()


def unpack_kernel(
    final,
    rows,
    row_out,
    down_out,
    up_out,
    cross_bias_out,
    h1_out,
    bias1_out,
    h2_out,
    bias2_out,
    logit_out,
):
    row_out[0] = rows[...]
    for k in range(Z):
        at = slice(128 * k, 128 * k + 128)
        h1_out[:, at] = final[0, k, :, :].astype(f32)[0:136]
        h2_out[:, at] = final[1, k, 0:64, :].astype(f32)
        up_out[:, at] = final[1, k, 64:80, :].astype(f32)
        up_out[:, 1024 + 128 * k : 1024 + 128 * k + 128] = final[1, k, 80:96, :].astype(f32)
    up_out[:, 2048:2176] = final[1, 6, 96:112, :].astype(f32)
    for k in range(2):
        at = slice(128 * k, 128 * k + 128)
        down_out[0:48, at] = final[1, k, 96:144, :].astype(f32)
        down_out[48:96, at] = final[1, 2 + k, 96:144, :].astype(f32)
        down_out[96:136, at] = final[1, 4 + k, 96:144, :].astype(f32)[0:40]
    low = final[1, 6, 112:128, :].astype(f32)
    high = final[1, 7, 112:128, :].astype(f32)
    cross_bias_out[pl.ds(0, 128)] = low[0]
    cross_bias_out[pl.ds(128, 8)] = high[0, 0:8]
    for k, one in enumerate((bias1_out, bias2_out, logit_out)):
        one[...] = low[k + 1, 0:64]


def unpack(final, rows):
    vmem = pl.BlockSpec(memory_space=pltpu.VMEM)
    shapes = ((1,) + rows.shape, (136, 256), (16, 2176), (136,), (136, 1024), (64,), (64, 1024))
    shapes += ((64,), (64,))
    return pl.pallas_call(
        unpack_kernel,
        out_shape=tuple(jax.ShapeDtypeStruct(shape, f32) for shape in shapes),
        in_specs=[vmem] * 2,
        out_specs=(vmem,) * 9,
        compiler_params=pltpu.CompilerParams(vmem_limit_bytes=16 << 20),
    )(final, rows)


def exchange(parts, sums):
    vmem = pl.BlockSpec(memory_space=pltpu.VMEM)
    rows, width = parts.shape[1:]
    half = rows // 2
    dma = pltpu.SemaphoreType.DMA
    return pl.pallas_call(
        exchange_kernel,
        out_shape=(
            jax.ShapeDtypeStruct((rows, width), f32),
            jax.ShapeDtypeStruct((2, Z, PIECE, 128), bf16),
        ),
        in_specs=[pl.BlockSpec(memory_space=pl.ANY), vmem],
        out_specs=(vmem,) * 2,
        scratch_shapes=[
            pltpu.VMEM((4, half, width), bf16),
            pltpu.VMEM((4, half, width), bf16),
            pltpu.VMEM((4, half, width), bf16),
            pltpu.VMEM((4, half, width), bf16),
            pltpu.VMEM((4, rows, width), bf16),
            pltpu.VMEM((4, rows, width), bf16),
            pltpu.VMEM((4, rows, width), bf16),
            pltpu.VMEM((2, half, width), bf16),
            pltpu.VMEM((2, rows, width), bf16),
            pltpu.VMEM((80, WIDE), bf16),
            pltpu.VMEM((64, WIDE), bf16),
            pltpu.VMEM((80, WIDE), bf16),
            pltpu.VMEM((64, WIDE), bf16),
            pltpu.VMEM((2, PIECE, WIDE), bf16),
            pltpu.VMEM((Z, PIECE, 128), bf16),
            pltpu.VMEM((Z - 1, PIECE, 128), bf16),
            pltpu.VMEM((4, rows, width), bf16),
            dma((3, 4)),
            dma((4, 6)),
            dma((4, 6)),
            dma((6,)),
            dma((6,)),
            dma((6,)),
            dma((6,)),
            dma((Z - 1,)),
            dma((Z - 1,)),
            dma((Z - 1,)),
            dma((Z - 1,)),
            dma,
            dma,
        ],
        compiler_params=pltpu.CompilerParams(
            collective_id=1, has_side_effects=True, vmem_limit_bytes=40 << 20
        ),
    )(parts, sums)


def scatter_kernel(slots_ref, values_ref, o_ref, s_ref, narrow, wide, sem, value_sem, *accs):
    count, width = narrow.shape
    slots = o_ref.shape[0]
    row = lax.axis_index("row")
    per_table = slots_ref.shape[1] // (2 * Z)
    own = per_table // (Y * X)
    values = pltpu.make_async_copy(values_ref, narrow, value_sem)
    values.start()

    def fetch(t):
        at = (t // 2) * per_table + row * own + (t % 2) * 128
        return pltpu.make_async_copy(
            slots_ref.at[:, pl.ds(pl.multiple_of(at, 128), 128)], s_ref.at[t], sem.at[t]
        )

    for t in range(count // 128):
        fetch(t).start()

    def clear(i, c):
        for acc in accs:
            acc[pl.ds(pl.multiple_of(i * 512, 512), 512), :] = jnp.zeros((512, width), f32)
        return c

    lax.fori_loop(0, slots // 512, clear, 0)
    values.wait()
    for t in range(count // 128):
        fetch(t).wait()

    def step(g, c):
        wide[...] = narrow[pl.ds(pl.multiple_of(g * 128, 128), 128), :].astype(f32)
        turn = 0
        for i in range(128):
            sample = wide[i : i + 1, :]
            for which in range(s_ref.shape[1]):
                acc = accs[turn % len(accs)]
                turn += 1
                at = pl.ds(s_ref[g, which, i], 1)
                acc[at, :] = acc[at, :] + sample
        return c

    lax.fori_loop(0, count // 128, step, 0)

    def finish(i, c):
        at = pl.ds(pl.multiple_of(i * 512, 512), 512)
        total = accs[0][at, :]
        for acc in accs[1:]:
            total = total + acc[at, :]
        o_ref[at, :] = total.astype(bf16)
        return c

    lax.fori_loop(0, slots // 512, finish, 0)


def scatter_rows(slots, values, total_slots):
    count, width = values.shape
    hot = slots.shape[0]
    anywhere = pl.BlockSpec(memory_space=pl.ANY)
    return pl.pallas_call(
        scatter_kernel,
        out_shape=pltpu.VMEM((total_slots, width), bf16),
        in_specs=[anywhere, anywhere],
        out_specs=pl.BlockSpec(memory_space=pltpu.VMEM),
        scratch_shapes=[
            pltpu.SMEM((count // 128, hot, 128), jnp.int32),
            pltpu.VMEM((count, width), bf16),
            pltpu.VMEM((128, width), f32),
            pltpu.SemaphoreType.DMA((count // 128,)),
            pltpu.SemaphoreType.DMA,
        ]
        + [pltpu.VMEM((total_slots, width), f32)] * 6,
        compiler_params=pltpu.CompilerParams(vmem_limit_bytes=50 << 20),
        cost_estimate=pl.CostEstimate(
            flops=10_000_000, bytes_accessed=100_000_000, transcendentals=0
        ),
    )(slots, values)


def local(
    dense_feat,
    pooled,
    labels,
    cross_down,
    cross_up,
    cross_bias,
    w_hidden1,
    bias1,
    w_hidden2,
    bias2,
    w_logit,
    lookup_slots,
):
    width = dense_feat.shape[1]
    n_row = lax.axis_size("row")
    u_shard = 1024
    big = (dense_feat, pooled, cross_down, cross_up, w_hidden1, w_hidden2)
    rows = [labels[None, :], cross_bias, bias1[None, :], bias2[None, :], w_logit[None, :]]
    received, sums = dense_part(big, rows)
    partial = scatter_rows(
        jnp.transpose(lookup_slots[0]), received.reshape(-1, width), n_row * u_shard
    )
    row_sums, final = exchange(partial.reshape(n_row, u_shard, width), sums)
    return tuple(unpack(final, row_sums))


def solution(mesh):
    in_specs = (
        P(("table", "row"), None),
        P(("table", "row"), None),
        P(("table", "row")),
        P(),
        P(),
        P(),
        P(),
        P(),
        P(),
        P(),
        P(),
        P("table", None, None),
    )
    out_specs = (
        P("table", "row", None),
        P("row", None),
        P("row", None),
        P("row"),
        P("row", None),
        P("row"),
        P("row", None),
        P("row"),
        P("row"),
    )
    return jax.shard_map(local, mesh=mesh, in_specs=in_specs, out_specs=out_specs, check_vma=False)
```

```python
import jax
import jax.numpy as jnp
from jax import lax
from jax.experimental import pallas as pl
from jax.experimental.pallas import tpu as pltpu
from jax.sharding import PartitionSpec as P

loss_scale = 16.0


MESH = pl.DeviceIdType.MESH
X, Y, Z = 4, 4, 8
PIECE = 144
WIDE = 1024
f32, bf16 = jnp.float32, jnp.bfloat16


def place():
    table = lax.axis_index("table")
    row = lax.axis_index("row")
    core, z = lax.rem(table, 2), table // 2
    y, x = row // X, lax.rem(row, X)
    return table, row, core, z, y, x


def slot_of(half, shard, y, x):
    dy = lax.rem(shard // X - y + Y, Y)
    dx = lax.rem(lax.rem(shard, X) - x + X, X)
    return dx * 4 + dy if half == 0 else dy * 4 + dx


def shard_of(core, y, x, first, second):
    dx = first * (1 - core) + second * core
    dy = second * (1 - core) + first * core
    return lax.rem(y + dy, Y) * X + lax.rem(x + dx, X)


def transposed(dst, src):
    for i in range(src.shape[1] // 128):
        at = slice(128 * i, 128 * i + 128)
        dst[at, :] = src[:, at].T


def ring(chunk, cut, size, vias, accs, gots, send, recv, plus, minus):
    low, high = pl.ds(0, cut), pl.ds(cut, size - cut)
    pairs = (
        (lambda: chunk(2).at[low], vias[0], plus),
        (lambda: chunk(2).at[high], vias[1], minus),
        (lambda: chunk(1).at[high], gots[0].at[high], plus),
        (lambda: chunk(3).at[low], gots[1].at[low], minus),
        (lambda: accs[0], gots[0].at[low], plus),
        (lambda: accs[1], gots[1].at[high], minus),
    )

    def copy(k):
        src, dst, who = pairs[k]
        return remote(src(), dst, send.at[k], recv.at[k], who)

    return copy


def remote(src, dst, s, r, who):
    return pltpu.make_async_remote_copy(
        src_ref=src, dst_ref=dst, send_sem=s, recv_sem=r, device_id=who, device_id_type=MESH
    )


def go(copies, *which):
    for k in which:
        copies(k).start()


def arrived(copies, *which):
    for k in which:
        copies(k).wait_recv()


def dot(a, b):
    return jnp.dot(a, b, preferred_element_type=f32)


def dot_t(a, b):
    return lax.dot_general(a, b, (((1,), (1,)), ((), ())), preferred_element_type=f32)


def tiles(body, width):
    for i in range(width // 256):
        body(slice(256 * i, 256 * i + 256), i)
    if width % 256:
        body(slice(width - width % 256, width), width // 256)


def dense_kernel(
    dense_feat,
    pooled,
    cross_down,
    cross_up,
    w_hidden1,
    w_hidden2,
    labels,
    cross_bias,
    bias1,
    bias2,
    w_logit,
    received,
    out,
    stacked,
    down_w,
    up_w,
    w1,
    w2,
    wide_plus,
    crossed,
    slope1,
    slope2,
    act_first,
    act_second,
    delta_second,
    delta_first,
    delta_crossed,
    delta_widened,
    reduced,
    delta_reduced,
    grad_logit,
    ready,
    packed,
    landed,
    flipped,
    small,
    via_plus,
    via_minus,
    got_plus,
    got_minus,
    load_sem,
    tsend,
    trecv,
    send_sem,
    recv_sem,
    send1,
    recv1,
    own_sem,
):
    table, row, core, z, y, x = place()
    n_table = 2 * Z
    other = z * 2 + 1 - core

    loads = [
        pltpu.make_async_copy(dense_feat, stacked.at[:, pl.ds(0, 128)], load_sem.at[0]),
        pltpu.make_async_copy(pooled, stacked.at[:, pl.ds(128, 2048)], load_sem.at[1]),
        pltpu.make_async_copy(cross_down, down_w, load_sem.at[2]),
        pltpu.make_async_copy(cross_up, up_w, load_sem.at[3]),
    ]
    for k in range(4):
        part = pl.ds(544 * k, 544)
        loads.append(pltpu.make_async_copy(w_hidden1.at[part], w1.at[part], load_sem.at[4 + k]))
    for k in range(2):
        part = pl.ds(512 * k, 512)
        loads.append(pltpu.make_async_copy(w_hidden2.at[part], w2.at[part], load_sem.at[8 + k]))
    for one in loads:
        one.start()

    def first_peer(d):
        return (table, shard_of(core, y, x, d, 0))

    barrier = pltpu.get_barrier_semaphore()
    for d in range(1, n_table):
        who = (lax.rem(table + d, n_table), row)
        pl.semaphore_signal(barrier, inc=1, device_id=who, device_id_type=MESH)
    for d in (1, 3):
        pl.semaphore_signal(barrier, inc=1, device_id=first_peer(d), device_id_type=MESH)

    def exchange_table(d):
        to = lax.rem(table + d, n_table)
        return remote(
            ready.at[to + 1], received.at[table], tsend.at[d - 1], trecv.at[d - 1], (to, row)
        )

    def came_table(d):
        came = lax.rem(table - d + n_table, n_table)
        return remote(
            ready.at[came + 1], received.at[came], tsend.at[d - 1], trecv.at[d - 1], (came, row)
        )

    def own_table():
        return pltpu.make_async_copy(ready.at[table + 1], received.at[table], own_sem)

    for k in (0, 1, 2):
        loads[k].wait()
    reduced[...] = dot(stacked[...], down_w[...]).astype(bf16)
    loads[3].wait()

    def cross(at, i):
        widened = dot(reduced[...], up_w[:, at]) + cross_bias[at][None, :]
        base = stacked[:, at].astype(f32)
        crossed[:, at] = (base * widened + base).astype(bf16)
        wide_plus[:, at] = widened + 1.0

    tiles(cross, 2176)
    for k in range(4, 8):
        loads[k].wait()

    def first_layer(at, i):
        pre = dot(crossed[...], w1[:, at]) + bias1[:, at]
        sig = jax.nn.sigmoid(pre)
        act_first[:, at] = (pre * sig).astype(bf16)
        slope1[:, at] = sig * (1.0 + pre * (1.0 - sig))

    tiles(first_layer, 1024)
    for k in range(8, 10):
        loads[k].wait()

    def second_layer(at, logits):
        pre = dot(act_first[...], w2[:, at]) + bias2[:, at]
        sig = jax.nn.sigmoid(pre)
        act = (pre * sig).astype(bf16)
        act_second[:, at] = act
        slope2[:, at] = sig * (1.0 + pre * (1.0 - sig))
        return logits + jnp.sum(act.astype(f32) * w_logit[:, at], axis=1, keepdims=True)

    logits = jnp.zeros((256, 1), f32)
    for i in range(1024 // 256):
        logits = second_layer(slice(256 * i, 256 * i + 256), logits)
    same = lax.broadcasted_iota(jnp.int32, (256, 256), 0) == lax.broadcasted_iota(
        jnp.int32, (256, 256), 1
    )
    label = jnp.sum(jnp.where(same, labels[...].astype(f32), 0.0), axis=1, keepdims=True)
    delta_logit = loss_scale * (jax.nn.sigmoid(logits) - label)

    def back_second(at, i):
        delta_second[:, at] = (delta_logit * w_logit[:, at] * slope2[:, at]).astype(bf16)
        grad_logit[:, at] = jnp.sum(
            act_second[:, at].astype(f32) * delta_logit, axis=0, keepdims=True
        )

    tiles(back_second, 1024)

    def back_first(at, i):
        back = dot_t(delta_second[...], w2[at, :])
        delta_first[:, at] = (back * slope1[:, at]).astype(bf16)

    tiles(back_first, 1024)

    def back_cross(at, i):
        delta = dot_t(delta_first[...], w1[at, :])
        delta_crossed[:, at] = delta
        delta_widened[:, at] = (delta * stacked[:, at].astype(f32)).astype(bf16)

    tiles(back_cross, 2176)
    delta_reduced[...] = dot_t(delta_widened[...], up_w[...]).astype(bf16)

    def back_stacked(at, i):
        delta = delta_crossed[:, at] * wide_plus[:, at] + dot_t(delta_reduced[...], down_w[at, :])
        for k in range(delta.shape[1] // 128):
            ready[2 * i + k] = delta[:, 128 * k : 128 * k + 128].astype(bf16)

    tiles(back_stacked, 2176)
    pl.semaphore_wait(barrier, n_table + 1)
    for d in sorted(range(1, n_table), key=lambda d: (abs(d - Z), d)):
        exchange_table(d).start()
    own_table().start()

    def copy(half, slot):
        return remote(
            packed.at[half, slot], landed.at[slot], send_sem.at[slot], recv_sem.at[slot], (other, row)
        )

    transposed(flipped, act_first)

    def second(i, c):
        m = dot(flipped[slice(256 * i, 256 * i + 256), :], delta_second[...])
        for k in range(4):
            packed[1, slot_of(1, i * 4 + k, y, x), 0:64, :] = m[64 * k : 64 * k + 64].astype(bf16)
        return c

    for i in range(4):
        second(i, 0)

    transposed(small, reduced)

    def up(i, c):
        left = small[slice(64 * i, 64 * i + 64), :]
        m0 = dot(left, delta_widened[:, 0:1024])
        m1 = dot(left, delta_widened[:, 1024:2048])
        m2 = dot(left, delta_widened[:, 2048:2176])
        for k in range(4):
            slot = slot_of(1, i * 4 + k, y, x)
            part = slice(16 * k, 16 * k + 16)
            packed[1, slot, 64:80, :] = m0[part].astype(bf16)
            packed[1, slot, 80:96, :] = m1[part].astype(bf16)
            packed[1, slot, 96:112, 768:896] = m2[part].astype(bf16)
            packed[1, slot, 96:112, 896:1024] = jnp.zeros((16, 128), bf16)
            packed[1, slot, 128:144, 768:1024] = jnp.zeros((16, 256), bf16)
        return c

    for i in range(4):
        up(i, 0)

    transposed(flipped, stacked)

    def down(i, c):
        m = dot(flipped[slice(272 * i, 272 * i + 272), :], delta_reduced[...])
        for k in range(2):
            slot = slot_of(1, i * 2 + k, y, x)
            d = m[136 * k : 136 * k + 136]
            packed[1, slot, 96:144, 0:256] = d[0:48].astype(bf16)
            packed[1, slot, 96:144, 256:512] = d[48:96].astype(bf16)
            last = jnp.concatenate([d[96:136], jnp.zeros((8, 256), f32)], axis=0)
            packed[1, slot, 96:144, 512:768] = last.astype(bf16)
        return c

    for i in range(8):
        down(i, 0)

    ones = jnp.ones((8, 256), bf16)
    wide_sums = dot(ones, delta_widened[...])
    which = lax.broadcasted_iota(jnp.int32, (8, 1024), 0)
    sums = jnp.where(which == 1, dot(ones, delta_first[...]), dot(ones, delta_second[...]))
    sums = jnp.where(which == 3, grad_logit[...], sums)
    first_row = which[:, 0:256] == 0
    for shard in range(16):
        a = wide_sums if shard == 0 else pltpu.roll(wide_sums, 2176 - 136 * shard, 1)
        b = sums if shard == 0 else pltpu.roll(sums, 1024 - 64 * shard, 1)
        block = jnp.where(first_row, a[:, 0:256], b[:, 0:256])
        block = jnp.concatenate([block, jnp.zeros((8, 256), f32)], axis=0).astype(bf16)
        packed[1, slot_of(1, shard, y, x), 112:128, 768:1024] = block

    order = (8, 9, 10, 11, 4, 12, 5, 13, 6, 14, 7, 15, 0, 1, 2, 3)

    @pl.when(core == 0)
    def _():
        for slot in order:
            copy(1, slot).start()

    transposed(flipped, crossed)

    def first(i, c):
        m = dot(flipped[slice(272 * i, 272 * i + 272), :], delta_first[...])
        for k in range(2):
            slot = slot_of(0, i * 2 + k, y, x)
            d = jnp.concatenate([m[136 * k : 136 * k + 136], jnp.zeros((8, WIDE), f32)], axis=0)
            packed[0, slot] = d.astype(bf16)
        return c

    for i in range(8):
        first(i, 0)

    @pl.when(core == 1)
    def _():
        for slot in order:
            copy(0, slot).start()

    cut = 80

    def ring1(j):
        return ring(
            lambda d: packed.at[core, d * 4 + j],
            cut,
            PIECE,
            (via_plus.at[j], via_minus.at[j]),
            (packed.at[core, 4 + j, pl.ds(0, cut)], packed.at[core, 12 + j, pl.ds(cut, PIECE - cut)]),
            (got_plus.at[j], got_minus.at[j]),
            send1.at[j],
            recv1.at[j],
            first_peer(1),
            first_peer(3),
        )

    def add_pair(slot):
        copy(1 - core, slot).wait_recv()
        packed[core, slot] = (packed[core, slot].astype(f32) + landed[slot].astype(f32)).astype(bf16)

    def go_far(j, c):
        add_pair(8 + j)
        go(ring1(j), 0, 1)
        return c

    lax.fori_loop(0, 4, go_far, 0)

    def go_near(j, c):
        add_pair(4 + j)
        go(ring1(j), 2)
        add_pair(12 + j)
        go(ring1(j), 3)
        return c

    lax.fori_loop(0, 4, go_near, 0)

    def go_on(j, c):
        arrived(ring1(j), 0, 1)
        low, high = pl.ds(0, cut), pl.ds(cut, PIECE - cut)
        packed[core, 4 + j, low] = (
            packed[core, 4 + j, low].astype(f32) + via_plus[j].astype(f32)
        ).astype(bf16)
        packed[core, 12 + j, high] = (
            packed[core, 12 + j, high].astype(f32) + via_minus[j].astype(f32)
        ).astype(bf16)
        go(ring1(j), 4, 5)
        return c

    lax.fori_loop(0, 4, go_on, 0)

    def keep(j, c):
        add_pair(j)
        return c

    lax.fori_loop(0, 4, keep, 0)

    def finish(j, c):
        arrived(ring1(j), 2, 3, 4, 5)
        total = packed[core, j].astype(f32) + got_plus[j].astype(f32) + got_minus[j].astype(f32)
        out[j] = total.astype(bf16)
        return c

    lax.fori_loop(0, 4, finish, 0)

    def drain(slot, c):
        copy(1 - core, slot).wait_send()
        return c

    lax.fori_loop(0, 16, drain, 0)

    def drain1(j, c):
        for k in range(6):
            ring1(j)(k).wait_send()
        return c

    lax.fori_loop(0, 4, drain1, 0)
    own_table().wait()
    for d in range(1, n_table):
        came_table(d).wait_recv()
        exchange_table(d).wait_send()


def dense_part(big, rows):
    vmem = pl.BlockSpec(memory_space=pltpu.VMEM)
    anywhere = pl.BlockSpec(memory_space=pl.ANY)
    n_table = 2 * Z
    dma = pltpu.SemaphoreType.DMA
    return pl.pallas_call(
        dense_kernel,
        out_shape=(
            jax.ShapeDtypeStruct((n_table, 256, 128), bf16),
            jax.ShapeDtypeStruct((4, PIECE, WIDE), bf16),
        ),
        in_specs=[anywhere] * 6 + [vmem] * 5,
        out_specs=(anywhere, vmem),
        scratch_shapes=[
            pltpu.VMEM((256, 2176), bf16),
            pltpu.VMEM((2176, 256), bf16),
            pltpu.VMEM((256, 2176), bf16),
            pltpu.VMEM((2176, 1024), bf16),
            pltpu.VMEM((1024, 1024), bf16),
            pltpu.VMEM((256, 2176), f32),
            pltpu.VMEM((256, 2176), bf16),
            pltpu.VMEM((256, 1024), f32),
            pltpu.VMEM((256, 1024), f32),
            pltpu.VMEM((256, 1024), bf16),
            pltpu.VMEM((256, 1024), bf16),
            pltpu.VMEM((256, 1024), bf16),
            pltpu.VMEM((256, 1024), bf16),
            pltpu.VMEM((256, 2176), f32),
            pltpu.VMEM((256, 2176), bf16),
            pltpu.VMEM((256, 256), bf16),
            pltpu.VMEM((256, 256), bf16),
            pltpu.VMEM((1, 1024), f32),
            pltpu.VMEM((n_table + 1, 256, 128), bf16),
            pltpu.VMEM((2, 16, PIECE, WIDE), bf16),
            pltpu.VMEM((16, PIECE, WIDE), bf16),
            pltpu.VMEM((2176, 256), bf16),
            pltpu.VMEM((256, 256), bf16),
            pltpu.VMEM((4, 80, WIDE), bf16),
            pltpu.VMEM((4, 64, WIDE), bf16),
            pltpu.VMEM((4, PIECE, WIDE), bf16),
            pltpu.VMEM((4, PIECE, WIDE), bf16),
            dma((10,)),
            dma((n_table - 1,)),
            dma((n_table - 1,)),
            dma((16,)),
            dma((16,)),
            dma((4, 6)),
            dma((4, 6)),
            dma,
        ],
        compiler_params=pltpu.CompilerParams(
            collective_id=0, has_side_effects=True, vmem_limit_bytes=58 << 20
        ),
    )(*big, *rows)


def blocks(count, size, body):
    for i in range(count):
        body(slice(i * size, i * size + size))


def exchange_kernel(
    parts,
    dense_mid,
    row_out,
    final,
    via_plus,
    via_minus,
    acc_plus,
    acc_minus,
    got_plus,
    got_minus,
    mid,
    via2,
    got2,
    dense_via_plus,
    dense_via_minus,
    dense_acc_plus,
    dense_acc_minus,
    dense_got,
    zparts,
    zgot,
    own,
    own_sem,
    send1,
    recv1,
    send2,
    recv2,
    wsend,
    wrecv,
    zsend,
    zrecv,
    gsend,
    grecv,
    csend,
    crecv,
):
    table, row, core, z, y, x = place()
    sibling = z * 2 + 1 - core
    rows = parts.shape[1]

    def first_peer(d):
        return (table, shard_of(core, y, x, d, 0))

    def second_peer(j):
        return (table, shard_of(core, y, x, 0, j))

    def z_peer(d):
        return (lax.rem(z + d, Z) * 2 + core, row)

    barrier = pltpu.get_barrier_semaphore()
    peers = [first_peer(1), first_peer(3), second_peer(1), second_peer(3)]
    peers += [z_peer(d) for d in range(1, Z)] + [(sibling, row)]
    for who in peers:
        pl.semaphore_signal(barrier, inc=1, device_id=who, device_id_type=MESH)
    pl.semaphore_wait(barrier, len(peers))

    half = rows // 2
    far_first = (4, 3, 5, 2, 6, 1, 7)

    def ring1(j):
        return ring(
            lambda d: parts.at[shard_of(core, y, x, d, j)],
            half,
            rows,
            (via_plus.at[j], via_minus.at[j]),
            (acc_plus.at[j], acc_minus.at[j]),
            (got_plus.at[j], got_minus.at[j]),
            send1.at[j],
            recv1.at[j],
            first_peer(1),
            first_peer(3),
        )

    def ring2():
        return ring(
            lambda d: mid.at[d],
            half,
            rows,
            (via2.at[0], via2.at[1]),
            (mid.at[1, pl.ds(0, half)], mid.at[3, pl.ds(half, half)]),
            (got2.at[0], got2.at[1]),
            send2,
            recv2,
            second_peer(1),
            second_peer(3),
        )

    cut = 80

    def ringw():
        return ring(
            lambda d: dense_mid.at[d],
            cut,
            PIECE,
            (dense_via_plus, dense_via_minus),
            (dense_acc_plus, dense_acc_minus),
            (dense_got.at[0], dense_got.at[1]),
            wsend,
            wrecv,
            second_peer(1),
            second_peer(3),
        )

    def copyz(d):
        return remote(
            zparts.at[lax.rem(z + d, Z)], zgot.at[d - 1], zsend.at[d - 1], zrecv.at[d - 1], z_peer(d)
        )

    def copyg(d, which):
        piece = final.at[core, which]
        return remote(piece, piece, gsend.at[d - 1], grecv.at[d - 1], z_peer(d))

    def copyc(half):
        return remote(final.at[half], final.at[half], csend, crecv, (sibling, row))

    def add_up(*terms):
        total = terms[0].astype(f32)
        for term in terms[1:]:
            total = total + term.astype(f32)
        return total

    def local(k, j):
        src, dst = (
            (parts.at[shard_of(core, y, x, 1, j), pl.ds(0, half)], acc_plus.at[j]),
            (parts.at[shard_of(core, y, x, 3, j), pl.ds(half, half)], acc_minus.at[j]),
            (parts.at[shard_of(core, y, x, 0, j)], own.at[j]),
        )[k]
        return pltpu.make_async_copy(src, dst, own_sem.at[k, j])

    def forward(j):
        copies = ring1(j)
        local(0, j).wait()
        arrived(copies, 0)

        def plus(at):
            acc_plus[j, at, :] = add_up(acc_plus[j, at, :], via_plus[j, at, :]).astype(bf16)

        blocks(half // 128, 128, plus)
        go(copies, 4)
        local(1, j).wait()
        arrived(copies, 1)

        def minus(at):
            acc_minus[j, at, :] = add_up(acc_minus[j, at, :], via_minus[j, at, :]).astype(bf16)

        blocks(half // 128, 128, minus)
        go(copies, 5)

    def row_mid(j):
        local(2, j).wait()
        arrived(ring1(j), 2, 3, 4, 5)

        def block(at):
            total = add_up(own[j, at, :], got_plus[j, at, :], got_minus[j, at, :])
            mid[j, at, :] = total.astype(bf16)

        blocks(rows // 128, 128, block)

    go(ringw(), 0, 1)
    go(ring1(2), 0, 1)
    go(ringw(), 2, 3)
    go(ring1(2), 2, 3)
    go(ring1(1), 0, 1)
    for j in (2, 1, 3, 0):
        for k in range(3):
            local(k, j).start()
    arrived(ringw(), 0, 1)

    def dense_plus(at):
        dense_acc_plus[at, :] = add_up(dense_mid[1, at, :], dense_via_plus[at, :]).astype(bf16)

    def dense_minus(at):
        later = slice(cut + at.start, cut + at.stop)
        dense_acc_minus[at, :] = add_up(dense_mid[3, later, :], dense_via_minus[at, :]).astype(bf16)

    blocks(cut // 16, 16, dense_plus)
    blocks((PIECE - cut) // 16, 16, dense_minus)
    go(ringw(), 4, 5)
    forward(2)
    go(ring1(1), 2, 3)
    go(ring1(3), 0, 1)
    forward(1)
    go(ring1(3), 2, 3)
    go(ring1(0), 0, 1)
    arrived(ringw(), 2, 3, 4, 5)

    def dense_last(at):
        total = add_up(dense_mid[0, at, :], dense_got[0, at, :], dense_got[1, at, :]).astype(bf16)
        for k in range(Z):
            zparts[k, at, :] = total[:, 128 * k : 128 * k + 128]

    blocks(PIECE // 16, 16, dense_last)
    for d in far_first:
        copyz(d).start()
    forward(3)
    go(ring1(0), 2, 3)
    for d in range(1, Z):
        copyz(d).wait_recv()
    final[core, z] = add_up(zparts[z], *[zgot[d - 1] for d in range(1, Z)]).astype(bf16)
    for d in far_first:
        copyg(d, z).start()
    row_mid(2)
    go(ring2(), 0, 1)
    forward(0)
    row_mid(1)
    go(ring2(), 2)
    for d in range(1, Z):
        copyg(d, lax.rem(z - d + Z, Z)).wait_recv()
    copyc(core).start()
    row_mid(3)
    go(ring2(), 3)
    arrived(ring2(), 0, 1)

    def mid_add(at):
        later = slice(half + at.start, half + at.stop)
        mid[1, at, :] = add_up(mid[1, at, :], via2[0, at, :]).astype(bf16)
        mid[3, later, :] = add_up(mid[3, later, :], via2[1, at, :]).astype(bf16)

    blocks(half // 128, 128, mid_add)
    go(ring2(), 4, 5)
    copyc(1 - core).wait_recv()
    arrived(ring1(0), 2, 3, 4, 5)
    arrived(ring2(), 2, 3, 4, 5)

    local(2, 0).wait()

    def row_last(at):
        row_out[at, :] = add_up(
            own[0, at, :],
            got_plus[0, at, :],
            got_minus[0, at, :],
            got2[0, at, :],
            got2[1, at, :],
        )

    blocks(rows // 128, 128, row_last)

    for j in range(4):
        for k in range(6):
            ring1(j)(k).wait_send()
    for k in range(6):
        ring2()(k).wait_send()
        ringw()(k).wait_send()
    for d in range(1, Z):
        copyz(d).wait_send()
        copyg(d, z).wait_send()
    copyc(core).wait_send()


def unpack_kernel(
    final,
    rows,
    row_out,
    down_out,
    up_out,
    cross_bias_out,
    h1_out,
    bias1_out,
    h2_out,
    bias2_out,
    logit_out,
):
    row_out[0] = rows[...]
    for k in range(Z):
        at = slice(128 * k, 128 * k + 128)
        h1_out[:, at] = final[0, k, :, :].astype(f32)[0:136]
        h2_out[:, at] = final[1, k, 0:64, :].astype(f32)
        up_out[:, at] = final[1, k, 64:80, :].astype(f32)
        up_out[:, 1024 + 128 * k : 1024 + 128 * k + 128] = final[1, k, 80:96, :].astype(f32)
    up_out[:, 2048:2176] = final[1, 6, 96:112, :].astype(f32)
    for k in range(2):
        at = slice(128 * k, 128 * k + 128)
        down_out[0:48, at] = final[1, k, 96:144, :].astype(f32)
        down_out[48:96, at] = final[1, 2 + k, 96:144, :].astype(f32)
        down_out[96:136, at] = final[1, 4 + k, 96:144, :].astype(f32)[0:40]
    low = final[1, 6, 112:128, :].astype(f32)
    high = final[1, 7, 112:128, :].astype(f32)
    cross_bias_out[pl.ds(0, 128)] = low[0]
    cross_bias_out[pl.ds(128, 8)] = high[0, 0:8]
    for k, one in enumerate((bias1_out, bias2_out, logit_out)):
        one[...] = low[k + 1, 0:64]


def unpack(final, rows):
    vmem = pl.BlockSpec(memory_space=pltpu.VMEM)
    shapes = ((1,) + rows.shape, (136, 256), (16, 2176), (136,), (136, 1024), (64,), (64, 1024))
    shapes += ((64,), (64,))
    return pl.pallas_call(
        unpack_kernel,
        out_shape=tuple(jax.ShapeDtypeStruct(shape, f32) for shape in shapes),
        in_specs=[vmem] * 2,
        out_specs=(vmem,) * 9,
        compiler_params=pltpu.CompilerParams(vmem_limit_bytes=16 << 20),
    )(final, rows)


def exchange(parts, sums):
    vmem = pl.BlockSpec(memory_space=pltpu.VMEM)
    rows, width = parts.shape[1:]
    half = rows // 2
    dma = pltpu.SemaphoreType.DMA
    return pl.pallas_call(
        exchange_kernel,
        out_shape=(
            jax.ShapeDtypeStruct((rows, width), f32),
            jax.ShapeDtypeStruct((2, Z, PIECE, 128), bf16),
        ),
        in_specs=[pl.BlockSpec(memory_space=pl.ANY), vmem],
        out_specs=(vmem,) * 2,
        scratch_shapes=[
            pltpu.VMEM((4, half, width), bf16),
            pltpu.VMEM((4, half, width), bf16),
            pltpu.VMEM((4, half, width), bf16),
            pltpu.VMEM((4, half, width), bf16),
            pltpu.VMEM((4, rows, width), bf16),
            pltpu.VMEM((4, rows, width), bf16),
            pltpu.VMEM((4, rows, width), bf16),
            pltpu.VMEM((2, half, width), bf16),
            pltpu.VMEM((2, rows, width), bf16),
            pltpu.VMEM((80, WIDE), bf16),
            pltpu.VMEM((64, WIDE), bf16),
            pltpu.VMEM((80, WIDE), bf16),
            pltpu.VMEM((64, WIDE), bf16),
            pltpu.VMEM((2, PIECE, WIDE), bf16),
            pltpu.VMEM((Z, PIECE, 128), bf16),
            pltpu.VMEM((Z - 1, PIECE, 128), bf16),
            pltpu.VMEM((4, rows, width), bf16),
            dma((3, 4)),
            dma((4, 6)),
            dma((4, 6)),
            dma((6,)),
            dma((6,)),
            dma((6,)),
            dma((6,)),
            dma((Z - 1,)),
            dma((Z - 1,)),
            dma((Z - 1,)),
            dma((Z - 1,)),
            dma,
            dma,
        ],
        compiler_params=pltpu.CompilerParams(
            collective_id=1, has_side_effects=True, vmem_limit_bytes=40 << 20
        ),
    )(parts, sums)


def scatter_kernel(slots_ref, values_ref, o_ref, s_ref, narrow, wide, sem, value_sem, *accs):
    count, width = narrow.shape
    slots = o_ref.shape[0]
    row = lax.axis_index("row")
    per_table = slots_ref.shape[1] // (2 * Z)
    own = per_table // (Y * X)
    values = pltpu.make_async_copy(values_ref, narrow, value_sem)
    values.start()

    def fetch(t):
        at = (t // 2) * per_table + row * own + (t % 2) * 128
        return pltpu.make_async_copy(
            slots_ref.at[:, pl.ds(pl.multiple_of(at, 128), 128)], s_ref.at[t], sem.at[t]
        )

    for t in range(count // 128):
        fetch(t).start()

    def clear(i, c):
        for acc in accs:
            acc[pl.ds(pl.multiple_of(i * 512, 512), 512), :] = jnp.zeros((512, width), f32)
        return c

    lax.fori_loop(0, slots // 512, clear, 0)
    values.wait()
    for t in range(count // 128):
        fetch(t).wait()

    def step(g, c):
        wide[...] = narrow[pl.ds(pl.multiple_of(g * 128, 128), 128), :].astype(f32)
        turn = 0
        for i in range(128):
            sample = wide[i : i + 1, :]
            for which in range(s_ref.shape[1]):
                acc = accs[turn % len(accs)]
                turn += 1
                at = pl.ds(s_ref[g, which, i], 1)
                acc[at, :] = acc[at, :] + sample
        return c

    lax.fori_loop(0, count // 128, step, 0)

    def finish(i, c):
        at = pl.ds(pl.multiple_of(i * 512, 512), 512)
        total = accs[0][at, :]
        for acc in accs[1:]:
            total = total + acc[at, :]
        o_ref[at, :] = total.astype(bf16)
        return c

    lax.fori_loop(0, slots // 512, finish, 0)


def scatter_rows(slots, values, total_slots):
    count, width = values.shape
    hot = slots.shape[0]
    anywhere = pl.BlockSpec(memory_space=pl.ANY)
    return pl.pallas_call(
        scatter_kernel,
        out_shape=pltpu.VMEM((total_slots, width), bf16),
        in_specs=[anywhere, anywhere],
        out_specs=pl.BlockSpec(memory_space=pltpu.VMEM),
        scratch_shapes=[
            pltpu.SMEM((count // 128, hot, 128), jnp.int32),
            pltpu.VMEM((count, width), bf16),
            pltpu.VMEM((128, width), f32),
            pltpu.SemaphoreType.DMA((count // 128,)),
            pltpu.SemaphoreType.DMA,
        ]
        + [pltpu.VMEM((total_slots, width), f32)] * 6,
        compiler_params=pltpu.CompilerParams(vmem_limit_bytes=50 << 20),
        cost_estimate=pl.CostEstimate(
            flops=10_000_000, bytes_accessed=100_000_000, transcendentals=0
        ),
    )(slots, values)


def local(
    dense_feat,
    pooled,
    labels,
    cross_down,
    cross_up,
    cross_bias,
    w_hidden1,
    bias1,
    w_hidden2,
    bias2,
    w_logit,
    lookup_slots,
):
    width = dense_feat.shape[1]
    n_row = lax.axis_size("row")
    u_shard = 1024
    big = (dense_feat, pooled, cross_down, cross_up, w_hidden1, w_hidden2)
    rows = [labels[None, :], cross_bias, bias1[None, :], bias2[None, :], w_logit[None, :]]
    received, sums = dense_part(big, rows)
    partial = scatter_rows(
        jnp.transpose(lookup_slots[0]), received.reshape(-1, width), n_row * u_shard
    )
    row_sums, final = exchange(partial.reshape(n_row, u_shard, width), sums)
    return tuple(unpack(final, row_sums))


def solution(mesh):
    in_specs = (
        P(("table", "row"), None),
        P(("table", "row"), None),
        P(("table", "row")),
        P(),
        P(),
        P(),
        P(),
        P(),
        P(),
        P(),
        P(),
        P("table", None, None),
    )
    out_specs = (
        P("table", "row", None),
        P("row", None),
        P("row", None),
        P("row"),
        P("row", None),
        P("row"),
        P("row", None),
        P("row"),
        P("row"),
    )
    return jax.shard_map(local, mesh=mesh, in_specs=in_specs, out_specs=out_specs, check_vma=False)
```
